128 devices in a mesh: grp: 2 (over z_lo), tp: 8 (over y, z_hi), dp: 8 (over x, core).
Axes of the slice: x: 4, y: 4, z: 4 (z_hi: 2, z_lo: 2; z = z_hi * 2 + z_lo), core: 2. Of those that a mesh axis runs over, the one named last changes fastest.
Arguments:
- residual: bfloat16 [2, 512, 4096], P('grp', 'dp'), may hold values from -3 to 3
- norm_gain: bfloat16 [2, 4096], P('grp'), may hold values from 0.29882812 to 3
- w_query: bfloat16 [2, 4096, 4096], P('grp', 'dp', 'tp'), may hold values from -0.09375 to 0.09375
- w_key: bfloat16 [2, 4096, 1024], P('grp', 'dp', 'tp'), may hold values from -0.09375 to 0.09375
- w_value: bfloat16 [2, 4096, 1024], P('grp', 'dp', 'tp'), may hold values from -0.09375 to 0.09375
- w_output: bfloat16 [2, 4096, 4096], P('grp', 'tp', 'dp'), may hold values from -0.375 to 0.375
- doc_lengths: int32 [4], replicated, may hold values from 1 to 256, 512 in all
- coder_weight: bfloat16 [65536, 2, 4096], P(('grp', 'tp', 'dp')), may hold values from -0.0625 to 0.0625
- enc_bias: float32 [65536], P(('grp', 'tp', 'dp')), may hold values from -3 to 3
- dec_bias: float32 [2, 4096], replicated, may hold values from -3 to 3
Outputs:
- grad_weight: bfloat16 [65536, 2, 4096], P(('grp', 'tp', 'dp'))
- grad_enc_bias: float32 [65536], P(('grp', 'tp', 'dp'))
- grad_dec_bias: float32 [2, 4096], replicated
The draws below stay inside these ranges and needn't reach their ends.
Inputs may be any that keep to these rules, and one draw needn't show every extreme that they name: `doc_lengths`: 4 document lengths that add up to 512, one of them exactly 256.
All inputs are finite; a program needn't handle non-finite values.
Results may differ from the reference program's by a relative error of at most 0.007.
The reference program's roundings to bfloat16 on the way count: a program that leaves them out, or rounds other values in their place, can miss the bound.
Values may be sent and summed in bfloat16 or wider, within the bound.
A program may use at most 192 MiB of HBM per device.

```python
import math
import jax
import jax.numpy as jnp
import numpy as np
from jax import lax

D = 4096
HEADS = 32
KV_HEADS = 8
HEAD_DIM = 128
LAT_DEV = 512
DOCS = 4
TOKENS = 512
LATENTS = 65536


def shard_levels(stream_key, extent, shards, least, high):
    level = 1.0
    for dim, shards_of in shards:
        steps = jax.random.uniform(jax.random.fold_in(jax.random.fold_in(stream_key, 6), dim), (shards_of,), jnp.float32, least / len(shards), high / len(shards))
        level = level * jnp.repeat(jnp.exp(steps), extent[dim] // shards_of).reshape((-1,) + (1,) * (len(extent) - 1 - dim))
    return level


def length_profile(number_of, total, bound, lean):
    portions = [(1 << 20) // math.isqrt(rank ** lean) + 1 for rank in range(2, number_of + 1)]
    surplus, counts = total - bound - (number_of - 1), [1] * (number_of - 1)
    while surplus > 0:
        free = [i for i in range(number_of - 1) if counts[i] < bound]
        mass, left = sum([portions[i] for i in free]), surplus
        for i in free:
            addition = min(bound - counts[i], max(1, left * portions[i] // mass), surplus)
            counts[i] = counts[i] + addition
            surplus = surplus - addition
    return np.array([bound] + counts)


def uneven(own_key, count, total, bound, slope):
    if count == 2:
        one = jax.random.randint(own_key, (), max(1, total - bound), min(bound, total - 1) + 1)
        return jnp.stack([one, total - one])
    lengths = jnp.asarray(length_profile(count, total, bound, slope), jnp.int32)
    pairs = (count - 1) // 2
    source_of, taker = lengths[1:1 + 2 * pairs:2], lengths[2:2 + 2 * pairs:2]
    slack = jnp.minimum(source_of - 1, bound - taker)
    moved = jax.random.randint(jax.random.fold_in(own_key, 1), (pairs,), 0, 1 << 20) % (slack + 1)
    lengths = lengths.at[1:1 + 2 * pairs:2].set(source_of - moved).at[2:2 + 2 * pairs:2].set(taker + moved)
    return lengths[jax.random.permutation(jax.random.fold_in(own_key, 2), count)]


def centred(own_key, shape, spread, limit, pieces=(), kind=jnp.bfloat16):
    entries = spread * jax.random.normal(own_key, shape, jnp.float32)
    if pieces:
        entries = entries * shard_levels(own_key, shape, pieces, -0.22, 0.18)
    return jnp.clip(entries, -limit, limit).astype(kind)


def setup_inputs(seed: int = 0) -> dict:
    key_of = jax.random.split(jax.random.key(seed), 11)
    return {
        "residual": centred(key_of[0], (2, TOKENS, D), 0.5, 3.0, ((0, 2), (1, 8))),
        "norm_gain": jnp.clip(jnp.exp(math.log(3.0) - 2.306499 * jax.random.uniform(key_of[1], (2, D), jnp.float32) ** shard_levels(key_of[1], (2, D), ((0, 2),), -0.2, 0.2)), 0.29882812, 3.0).astype(jnp.bfloat16),
        "w_query": centred(key_of[2], (2, D, HEADS * HEAD_DIM), D ** -0.5, 0.09375, ((0, 2), (1, 8), (2, 8))),
        "w_key": centred(key_of[3], (2, D, KV_HEADS * HEAD_DIM), D ** -0.5, 0.09375, ((0, 2), (1, 8), (2, 8))),
        "w_value": centred(key_of[4], (2, D, KV_HEADS * HEAD_DIM), D ** -0.5, 0.09375, ((0, 2), (1, 8), (2, 8))),
        "w_output": centred(key_of[5], (2, HEADS * HEAD_DIM, D), (HEADS * HEAD_DIM // 16) ** -0.5, 0.375, ((0, 2), (1, 8), (2, 8))),
        "doc_lengths": uneven(key_of[6], DOCS, TOKENS, TOKENS // 2, 2).astype(jnp.int32),
        "coder_weight": centred(key_of[7], (LATENTS, 2, D), (2 * D) ** -0.5, 0.0625, ((0, 128),)),
        "enc_bias": centred(key_of[8], (LATENTS,), 0.5, 3.0, ((0, 128),), jnp.float32),
        "dec_bias": centred(key_of[9], (2, D), 0.5, 3.0, (), jnp.float32),
    }


sparsity = 1.0
rope_base = 500000.0

def doc_layout(doc_lengths, token_index):
    doc_ends = jnp.cumsum(doc_lengths).astype(jnp.int32)
    passed = (token_index[:, None] >= doc_ends[None, :]).astype(jnp.int32)
    doc_ids = lax.optimization_barrier(jnp.sum(passed, axis=1)).astype(jnp.int32)
    doc_start = lax.optimization_barrier(jnp.sum(passed * doc_lengths[None, :], axis=1)).astype(jnp.int32)
    return (doc_ids, (token_index - doc_start).astype(jnp.int32))

def rotate(values, position):
    half_dim = values.shape[-1] // 2
    inv_freq = rope_base ** (-jnp.arange(half_dim, dtype=jnp.float32) * 2.0 / values.shape[-1])
    angles = position.astype(jnp.float32)[:, None] * inv_freq[None, :]
    cosine = jnp.cos(angles)[:, None, :]
    sine_vals = jnp.sin(angles)[:, None, :]
    low_half = values[..., :half_dim]
    high_half = values[..., half_dim:]
    return jnp.concatenate([low_half * cosine - high_half * sine_vals, high_half * cosine + low_half * sine_vals], -1)

def gelu_pair(pre_act):
    normal_cdf = 0.5 * (1.0 + lax.erf(pre_act * 0.7071067811865476))
    density = jnp.exp(-0.5 * pre_act * pre_act) * 0.3989422804014327
    return (pre_act * normal_cdf, normal_cdf + pre_act * density)

def attend_layer(inputs, gain, w_query, w_key, w_value, w_output, doc_ids, position, token_index):
    inputs_wide = inputs.astype(jnp.float32)
    normed = (inputs_wide * lax.rsqrt(lax.optimization_barrier(jnp.mean(inputs_wide * inputs_wide, -1, keepdims=True)) + 1e-05) * gain.astype(jnp.float32)).astype(jnp.bfloat16)
    query = jnp.dot(normed, w_query, preferred_element_type=jnp.float32).reshape(TOKENS, HEADS, HEAD_DIM)
    keys_raw = jnp.dot(normed, w_key, preferred_element_type=jnp.float32).reshape(TOKENS, KV_HEADS, HEAD_DIM)
    values_bf = jnp.dot(normed, w_value, preferred_element_type=jnp.float32).astype(jnp.bfloat16).reshape(TOKENS, KV_HEADS, HEAD_DIM)
    group_size = HEADS // KV_HEADS
    query = rotate(query, position).astype(jnp.bfloat16).reshape(TOKENS, KV_HEADS, group_size, HEAD_DIM)
    keys_rot = rotate(keys_raw, position).astype(jnp.bfloat16)
    scores = jnp.einsum('qkgh,skh->kgqs', query.astype(jnp.float32), keys_rot.astype(jnp.float32)) * HEAD_DIM ** (-0.5)
    allowed = (doc_ids[:, None] == doc_ids[None, :]) & (token_index[None, :] <= token_index[:, None])
    exp_terms = jnp.where(allowed, jnp.exp(jnp.where(allowed, scores, 0.0)), 0.0)
    weights = (exp_terms / lax.optimization_barrier(jnp.sum(exp_terms, -1, keepdims=True))).astype(jnp.bfloat16)
    head_mixed = jnp.einsum('kgqs,skh->qkgh', weights.astype(jnp.float32), values_bf.astype(jnp.float32)).astype(jnp.bfloat16).reshape(TOKENS, HEADS * HEAD_DIM)
    attn_sum = jnp.dot(head_mixed, w_output, preferred_element_type=jnp.float32)
    return (inputs_wide + attn_sum).astype(jnp.bfloat16)

def reference(residual, norm_gain, w_query, w_key, w_value, w_output, doc_lengths, coder_weight, enc_bias, dec_bias):
    token_index = jnp.arange(TOKENS, dtype=jnp.int32)
    doc_ids, position = doc_layout(doc_lengths, token_index)
    rows = jnp.stack([attend_layer(residual[model_idx], norm_gain[model_idx], w_query[model_idx], w_key[model_idx], w_value[model_idx], w_output[model_idx], doc_ids, position, token_index) for model_idx in range(2)])
    rows_wide = rows.astype(jnp.float32)
    blocks = coder_weight.reshape(-1, LAT_DEV, 2, D)
    biases = enc_bias.reshape(-1, LAT_DEV)

    def forward(recon_sum, operands):
        weight, enc_part = operands
        pre_act = jnp.einsum('mtd,lmd->tl', rows_wide, weight.astype(jnp.float32)) + enc_part[None, :]
        latent_act, act_slope = gelu_pair(pre_act)
        recon_sum = recon_sum + jnp.einsum('tl,lmd->mtd', latent_act.astype(jnp.bfloat16).astype(jnp.float32), weight.astype(jnp.float32))
        return (recon_sum, pre_act)
    recon_sum, pre_blocks = lax.scan(forward, jnp.zeros((2, TOKENS, D), jnp.float32), (blocks, biases))
    error_rows = (recon_sum + dec_bias.astype(jnp.float32)[:, None, :] - rows_wide).astype(jnp.bfloat16)
    error_wide = error_rows.astype(jnp.float32)

    def backward(operands):
        weight, pre_act = operands
        weight_wide = weight.astype(jnp.float32)
        latent_act, act_slope = gelu_pair(pre_act)
        dec_norms = jnp.sqrt(lax.optimization_barrier(jnp.sum(weight_wide * weight_wide, -1)) + 1e-06)
        norm_total = lax.optimization_barrier(jnp.sum(dec_norms, -1))
        act_grad = 2.0 / TOKENS * jnp.einsum('mtd,lmd->tl', error_wide, weight_wide) + sparsity / TOKENS * norm_total[None, :]
        pre_grad = act_grad * act_slope
        weight_grad = 2.0 / TOKENS * jnp.einsum('tl,mtd->lmd', latent_act.astype(jnp.bfloat16).astype(jnp.float32), error_wide)
        weight_grad = weight_grad + jnp.einsum('tl,mtd->lmd', pre_grad.astype(jnp.bfloat16).astype(jnp.float32), rows_wide)
        weight_grad = weight_grad + sparsity / TOKENS * lax.optimization_barrier(jnp.sum(latent_act, 0))[:, None, None] * weight_wide / dec_norms[:, :, None]
        return (weight_grad.astype(jnp.bfloat16), lax.optimization_barrier(jnp.sum(pre_grad, 0)))
    grads, bias_grads = lax.map(backward, (blocks, pre_blocks))
    return (grads.reshape(LATENTS, 2, D), bias_grads.reshape(LATENTS), 2.0 / TOKENS * lax.optimization_barrier(jnp.sum(error_wide, 1)))
```

```python
import functools
import jax
import jax.numpy as jnp
from jax import lax
from jax.experimental import pallas as pl
from jax.experimental.pallas import tpu as pltpu
from jax.sharding import PartitionSpec as P

HEAD_DIM = 128
TOK_DEV = 64
TOKENS = 512
BLOCK = 512
HALF = BLOCK // 2
RING = 4

sparsity = 1.0
rope_base = 500000.0

ROUTES = (
    ((0, 32, "xyz"), (32, 16, "yzx"), (48, 16, "zxy")),
    ((0, 32, "yzx"), (32, 16, "xyz"), (48, 16, "zxy")),
)


class Place:
    def __init__(self):
        self.m = lax.axis_index("grp")
        tp, dp = lax.axis_index("tp"), lax.axis_index("dp")
        self.tp, self.dp = tp, dp
        self.core = lax.rem(dp, 2)
        self.at = {"x": lax.div(dp, 2), "y": lax.div(tp, 2), "z": lax.rem(tp, 2) * 2 + self.m}

    def device(self, at, core):
        z = at["z"]
        return (lax.rem(z, 2), at["y"] * 2 + lax.div(z, 2), at["x"] * 2 + core)

    def beside(self, axis, step):
        return lax.rem(self.at[axis] + (step + RING), RING)

    def neighbour(self, axis, step):
        return self.device({**self.at, axis: self.beside(axis, step)}, self.core)

    def sibling(self):
        return self.device(self.at, 1 - self.core)

    def enter(self):
        barrier = pltpu.get_barrier_semaphore()
        for axis in "xyz":
            for step in (1, -1):
                pl.semaphore_signal(barrier, inc=1, device_id=self.neighbour(axis, step), device_id_type=pl.DeviceIdType.MESH)
        pl.semaphore_signal(barrier, inc=1, device_id=self.sibling(), device_id_type=pl.DeviceIdType.MESH)
        pl.semaphore_wait(barrier, 7)


def part(buf, core, sel, rows, cols=(0, BLOCK)):
    index = [] if core is None else [core]
    z = sel.get("z")
    if z is None:
        index += [slice(None), slice(None)]
    elif isinstance(z, int):
        index += [z // 2, z % 2]
    else:
        index += [lax.div(z, 2), lax.rem(z, 2)]
    for axis in "yx":
        index.append(sel.get(axis, slice(None)))
    index += [pl.ds(*rows), pl.ds(*cols)]
    return buf.at[tuple(index)]


LOW, HIGH = (0, HALF), (HALF, HALF)


def send(src, dst, send_sem, recv_sem, device):
    copy = pltpu.make_async_remote_copy(
        src_ref=src, dst_ref=dst, send_sem=send_sem, recv_sem=recv_sem, device_id=device, device_id_type=pl.DeviceIdType.MESH
    )
    copy.start()
    return copy


def arrive(dst, sem, place):
    pltpu.make_async_remote_copy(
        src_ref=dst, dst_ref=dst, send_sem=sem, recv_sem=sem, device_id=place.sibling(), device_id_type=pl.DeviceIdType.MESH
    ).wait_recv()


def gather(place, core, buf, sems):
    send_sems, recv_sems, give_sems, take_sems = sems
    routes, other = ROUTES[core], ROUTES[1 - core]
    sibling = place.sibling()
    pending = []

    def sel_of(order, k, v):
        sel = {order[k]: v}
        for axis in order[k + 1 :]:
            sel[axis] = place.at[axis]
        return sel

    def give(i, j, sel, rows):
        ref = part(buf, core, sel, rows)
        pending.append(send(ref, ref, give_sems.at[i, j], take_sems.at[i, j], sibling))

    for i, (r0, n, order) in enumerate(routes):
        give(i, 9, dict(place.at), (r0, n))
    for k in range(3):
        for i, (r0, n, order) in enumerate(routes):
            ref = part(buf, core, sel_of(order, k, place.at[order[k]]), (r0, n))
            for j, step in enumerate((1, -1)):
                pending.append(send(ref, ref, send_sems.at[i, k, j], recv_sems.at[i, k, j], place.neighbour(order[k], step)))
        for i, (r0, n, order) in enumerate(routes):
            axis = order[k]
            for j, (step, cols) in enumerate(((1, LOW), (-1, HIGH))):
                sel = sel_of(order, k, place.beside(axis, -step))
                arrive(part(buf, core, sel, (r0, n)), recv_sems.at[i, k, j], place)
                ref = part(buf, core, sel, (r0, n), cols)
                pending.append(send(ref, ref, send_sems.at[i, k, 2 + j], recv_sems.at[i, k, 2 + j], place.neighbour(axis, step)))
                give(i, k * 3 + j, sel, (r0, n))
        for i, (r0, n, order) in enumerate(routes):
            sel = sel_of(order, k, place.beside(order[k], 2))
            for j, cols in enumerate((LOW, HIGH)):
                arrive(part(buf, core, sel, (r0, n), cols), recv_sems.at[i, k, 2 + j], place)
            give(i, k * 3 + 2, sel, (r0, n))
    for i, (r0, n, order) in enumerate(other):
        for k in range(3):
            for j, v in enumerate((-1, 1, 2)):
                arrive(part(buf, 1 - core, sel_of(order, k, place.beside(order[k], v)), (r0, n)), take_sems.at[i, k * 3 + j], place)
        arrive(part(buf, 1 - core, dict(place.at), (r0, n)), take_sems.at[i, 9], place)
    for copy in pending:
        copy.wait_send()


def spread(sel, i):
    at, rest = {}, i
    for axis in "xyz":
        if sel.get(axis) is None:
            at[axis] = lax.rem(rest, RING)
            rest = lax.div(rest, RING)
        else:
            at[axis] = sel[axis]
    z = at["z"]
    zh, zl = (z // 2, z % 2) if isinstance(z, int) else (lax.div(z, 2), lax.rem(z, 2))
    return zh, zl, at["y"], at["x"]


def scatter_sum(place, core, sums, landing, result, sems):
    send_sems, recv_sems = sems
    routes = ROUTES[core]
    pending = []

    def sel_of(order, k, v, done):
        sel = {order[k]: v}
        for axis in order[:k]:
            sel[axis] = done if done is not None else place.at[axis]
        return sel

    def add(order, k, target, slots, rows, cols, into_result):
        sel = sel_of(order, k, target, None)
        count = RING ** (2 - k)

        def step(i, carry):
            own = spread(sel, i)
            window = (pl.ds(*rows), pl.ds(*cols))
            total = sums[own + window].astype(jnp.float32)
            for slot in slots:
                total = total + landing[spread(sel_of(order, k, slot, 3), i) + window].astype(jnp.float32)
            if into_result:
                result[window] = total
            else:
                sums[own + window] = total.astype(jnp.bfloat16)
            return carry

        lax.fori_loop(0, count, step, 0)

    for k in range(3):
        for i, (r0, n, order) in enumerate(routes):
            axis = order[k]
            for j, (step, slot, v, cols) in enumerate(((1, 0, 2, LOW), (-1, 0, 2, HIGH), (1, 1, 1, HIGH), (-1, 2, -1, LOW))):
                src = part(sums, None, sel_of(order, k, place.beside(axis, v), None), (r0, n), cols)
                dst = part(landing, None, sel_of(order, k, slot, 3), (r0, n), cols)
                pending.append(send(src, dst, send_sems.at[i, k, j], recv_sems.at[i, k, j], place.neighbour(axis, step)))
        for i, (r0, n, order) in enumerate(routes):
            axis = order[k]
            for j, (step, slot, cols) in enumerate(((1, 1, LOW), (-1, 2, HIGH))):
                arrive(part(landing, None, sel_of(order, k, 0, 3), (r0, n), cols), recv_sems.at[i, k, j], place)
                add(order, k, place.beside(axis, step), (0,), (r0, n), cols, False)
                src = part(sums, None, sel_of(order, k, place.beside(axis, step), None), (r0, n), cols)
                dst = part(landing, None, sel_of(order, k, slot, 3), (r0, n), cols)
                pending.append(send(src, dst, send_sems.at[i, k, 4 + j], recv_sems.at[i, k, 4 + j], place.neighbour(axis, step)))
        for i, (r0, n, order) in enumerate(routes):
            for j, (slot, cols) in ((2, (1, HIGH)), (3, (2, LOW)), (4, (1, LOW)), (5, (2, HIGH))):
                arrive(part(landing, None, sel_of(order, k, slot, 3), (r0, n), cols), recv_sems.at[i, k, j], place)
            add(order, k, place.at[order[k]], (1, 2), (r0, n), (0, BLOCK), k == 2)
    for copy in pending:
        copy.wait_send()


def gelu_pair(pre_act):
    normal_cdf = 0.5 * (1.0 + lax.erf(pre_act * 0.7071067811865476))
    density = jnp.exp(-0.5 * pre_act * pre_act) * 0.3989422804014327
    return (pre_act * normal_cdf, normal_cdf + pre_act * density)


def nt(a, b):
    return lax.dot_general(a, b, (((1,), (1,)), ((), ())), preferred_element_type=jnp.float32)


def nn(a, b):
    return lax.dot_general(a, b, (((1,), (0,)), ((), ())), preferred_element_type=jnp.float32)


def chunk_of(k):
    mm, x, c = lax.div(k, 8), lax.rem(lax.div(k, 2), RING), lax.rem(k, 2)
    return mm, x, c, pl.ds(pl.multiple_of((x * 2 + c) * BLOCK, BLOCK), BLOCK)


def token_rows(buf, mm, x, c):
    return buf[c, :, mm, :, x].reshape(TOKENS, BLOCK)


def coder_kernel(
    own_ref, w_hbm, enc_ref, dec_ref,
    gw_hbm, genc_ref, gdec_ref,
    rows, errs, w, sums, give, taken, landing, result, total, act_t, act, slope, pre_t, norms, latsum, stage,
    w_sem, rows_send, rows_recv, rows_give, rows_take, errs_send, errs_recv, errs_give, errs_take,
    sum_send, sum_recv, pair_send, pair_recv, out_sem,
):
    place = Place()
    m, core = place.m, place.core
    load = pltpu.make_async_copy(w_hbm, w, w_sem)
    load.start()
    own = (lax.div(place.at["z"], 2), m, place.at["y"], place.at["x"])
    rows[(core,) + own] = own_ref[...]
    place.enter()
    for c in (0, 1):
        pl.when(core == c)(functools.partial(gather, place, c, rows, (rows_send, rows_recv, rows_give, rows_take)))
    load.wait()

    def norm_step(i, carry):
        at = pl.ds(pl.multiple_of(i * 16, 16), 16)
        for mm in (0, 1):
            wide = w[mm, at, :].astype(jnp.float32)
            norms[mm, at, :] = jnp.sqrt(jnp.sum(wide * wide, -1, keepdims=True) + 1e-06)
        return carry

    lax.fori_loop(0, TOKENS // 16, norm_step, 0)

    def contract(buf):
        total[...] = jnp.zeros_like(total)

        def step(k, carry):
            mm, x, c, cols = chunk_of(k)
            total[...] += nt(w[mm, :, cols], token_rows(buf, mm, x, c))
            return carry

        lax.fori_loop(0, 16, step, 0)

    contract(rows)
    for l0 in range(0, BLOCK, 128):
        at = pl.ds(l0, 128)
        lat, slope[at, :] = gelu_pair(total[at, :] + enc_ref[at, :])
        latsum[at, :] = jnp.sum(lat, -1, keepdims=True)
        act_t[at, :] = lat.astype(jnp.bfloat16)
        act[:, at] = lat.T.astype(jnp.bfloat16)

    pairs = []
    for k in range(8):
        mm, x = k // 4, k % 4
        cols = pl.ds(pl.multiple_of((x * 2 + 1 - core) * BLOCK, BLOCK), BLOCK)
        give[:, mm, :, x] = nn(act[...], w[mm, :, cols]).astype(jnp.bfloat16).reshape(2, RING, TOK_DEV, BLOCK)
        pairs.append(send(give.at[:, mm, :, x], taken.at[:, mm, :, x], pair_send.at[k], pair_recv.at[k], place.sibling()))
    for k in range(8):
        mm, x = k // 4, k % 4
        cols = pl.ds(pl.multiple_of((x * 2 + core) * BLOCK, BLOCK), BLOCK)
        here = nn(act[...], w[mm, :, cols])
        pairs[k].wait_recv()
        there = taken[:, mm, :, x].reshape(TOKENS, BLOCK).astype(jnp.float32)
        sums[:, mm, :, x] = (here + there).astype(jnp.bfloat16).reshape(2, RING, TOK_DEV, BLOCK)
    for copy in pairs:
        copy.wait_send()
    for c in (0, 1):
        pl.when(core == c)(functools.partial(scatter_sum, place, c, sums, landing, result, (sum_send, sum_recv)))
    bias = dec_ref[pl.ds(m * 8 + place.dp, 1), :]
    errs[(core,) + own] = (result[...] + bias - own_ref[...].astype(jnp.float32)).astype(jnp.bfloat16)
    for c in (0, 1):
        pl.when(core == c)(functools.partial(gather, place, c, errs, (errs_send, errs_recv, errs_give, errs_take)))

    contract(errs)
    for l0 in range(0, BLOCK, 128):
        at = pl.ds(l0, 128)
        norm_total = norms[0, at, :] + norms[1, at, :]
        pre_grad = (2.0 / TOKENS * total[at, :] + sparsity / TOKENS * norm_total) * slope[at, :]
        genc_ref[at, :] = jnp.sum(pre_grad, -1, keepdims=True)
        pre_t[at, :] = pre_grad.astype(jnp.bfloat16)

    def grad_step(k, carry):
        mm, x, c, cols = chunk_of(k)
        slot = lax.rem(k, 2)
        out = pltpu.make_async_copy(stage.at[slot], gw_hbm.at[mm, :, cols], out_sem.at[slot])
        pl.when(k >= 2)(out.wait)
        err = token_rows(errs, mm, x, c)
        scale = sparsity / TOKENS * latsum[...] / norms[mm]
        grad = 2.0 / TOKENS * nn(act_t[...], err) + nn(pre_t[...], token_rows(rows, mm, x, c))
        stage[slot] = (grad + scale * w[mm, :, cols].astype(jnp.float32)).astype(jnp.bfloat16)
        out.start()
        ones = jnp.ones((16, TOKENS), jnp.bfloat16)
        gdec_ref[pl.ds(mm, 1), cols] = 2.0 / TOKENS * nn(ones, err)[:1]
        return carry

    lax.fori_loop(0, 16, grad_step, 0)
    for slot in (0, 1):
        pltpu.make_async_copy(stage.at[slot], gw_hbm.at[1, :, pl.ds((6 + slot) * BLOCK, BLOCK)], out_sem.at[slot]).wait()


def coder(own_rows, weight, enc_bias, dec_bias):
    latents, features = weight.shape[1:]
    blocks = (2, 2, RING, RING, TOK_DEV, BLOCK)
    bf16, f32 = jnp.bfloat16, jnp.float32
    dma = pltpu.SemaphoreType.DMA
    vmem = pl.BlockSpec(memory_space=pltpu.VMEM)
    hbm = pl.BlockSpec(memory_space=pl.ANY)
    ring = [dma((3, 3, 4)), dma((3, 3, 4)), dma((3, 10)), dma((3, 10))]
    return pl.pallas_call(
        coder_kernel,
        out_shape=(
            jax.ShapeDtypeStruct((2, latents, features), bf16),
            jax.ShapeDtypeStruct((latents, 1), f32),
            jax.ShapeDtypeStruct((2, features), f32),
        ),
        in_specs=[vmem, hbm, vmem, vmem],
        out_specs=(hbm, vmem, vmem),
        scratch_shapes=[
            pltpu.VMEM((2,) + blocks, bf16),
            pltpu.VMEM((2,) + blocks, bf16),
            pltpu.VMEM((2, latents, features), bf16),
            pltpu.VMEM(blocks, bf16),
            pltpu.VMEM(blocks, bf16),
            pltpu.VMEM(blocks, bf16),
            pltpu.VMEM(blocks, bf16),
            pltpu.VMEM((TOK_DEV, BLOCK), f32),
            pltpu.VMEM((latents, TOKENS), f32),
            pltpu.VMEM((latents, TOKENS), bf16),
            pltpu.VMEM((TOKENS, latents), bf16),
            pltpu.VMEM((latents, TOKENS), f32),
            pltpu.VMEM((latents, TOKENS), bf16),
            pltpu.VMEM((2, latents, 1), f32),
            pltpu.VMEM((latents, 1), f32),
            pltpu.VMEM((2, latents, BLOCK), bf16),
            dma(()),
            *ring,
            *ring,
            dma((3, 3, 6)),
            dma((3, 3, 6)),
            dma((8,)),
            dma((8,)),
            dma((2,)),
        ],
        compiler_params=pltpu.CompilerParams(collective_id=0, has_side_effects=True, vmem_limit_bytes=60 * 1024 * 1024),
        cost_estimate=pl.CostEstimate(flops=10 * TOKENS * latents * 2 * features, bytes_accessed=32 << 20, transcendentals=0),
    )(own_rows, weight, enc_bias.reshape(latents, 1), dec_bias.reshape(16, BLOCK))


def doc_layout(doc_lengths, token_index):
    doc_ends = jnp.cumsum(doc_lengths)
    passed = (token_index[:, None] >= doc_ends[None, :]).astype(jnp.int32)
    doc_ids = jnp.sum(passed, axis=1)
    doc_start = jnp.sum(passed * doc_lengths[None, :], axis=1)
    return (doc_ids, token_index - doc_start)


def rotate(values, position):
    half_dim = values.shape[-1] // 2
    inv_freq = rope_base ** (-jnp.arange(half_dim, dtype=jnp.float32) * 2.0 / values.shape[-1])
    angles = position.astype(jnp.float32)[:, None] * inv_freq[None, :]
    cosine = jnp.cos(angles)[:, None, :]
    sine_vals = jnp.sin(angles)[:, None, :]
    low_half = values[..., :half_dim]
    high_half = values[..., half_dim:]
    return jnp.concatenate(
        [low_half * cosine - high_half * sine_vals, high_half * cosine + low_half * sine_vals], -1
    )


def shards(
    residual,
    norm_gain,
    w_query,
    w_key,
    w_value,
    w_output,
    doc_lengths,
    coder_weight,
    enc_bias,
    dec_bias,
):
    dp_count = lax.axis_size("dp")
    tokens_all = dp_count * TOK_DEV
    dp_here = lax.axis_index("dp")
    own_index = dp_here * TOK_DEV + jnp.arange(TOK_DEV, dtype=jnp.int32)
    key_index = jnp.arange(tokens_all, dtype=jnp.int32)
    own_doc, own_pos = doc_layout(doc_lengths, own_index)
    key_doc, key_pos = doc_layout(doc_lengths, key_index)
    inputs = residual[0]
    inputs_wide = inputs.astype(jnp.float32)
    normed = (
        inputs_wide
        * lax.rsqrt(jnp.mean(inputs_wide * inputs_wide, -1, keepdims=True) + 1e-05)
        * norm_gain[0].astype(jnp.float32)
    ).astype(jnp.bfloat16)
    query_cols = w_query.shape[2]
    key_cols = w_key.shape[2]
    moved_rows, moved_normed = (
        lax.all_to_all(inputs, "dp", split_axis=1, concat_axis=0, tiled=True),
        lax.all_to_all(normed, "dp", split_axis=1, concat_axis=0, tiled=True),
    )
    joined = jnp.concatenate([w_query[0], w_key[0], w_value[0]], 1)
    summed = lax.psum_scatter(
        jnp.dot(moved_normed, joined, preferred_element_type=jnp.float32),
        "dp",
        scatter_dimension=0,
        tiled=True,
    )
    query_sum = summed[:, :query_cols]
    keys_sum = summed[:, query_cols : query_cols + key_cols]
    values_sum = summed[:, query_cols + key_cols :]
    heads_here = query_cols // HEAD_DIM
    kv_here = key_cols // HEAD_DIM
    group_size = heads_here // kv_here
    query_rot = (
        rotate(query_sum.reshape(TOK_DEV, heads_here, HEAD_DIM), own_pos)
        .astype(jnp.bfloat16)
        .reshape(TOK_DEV, kv_here, group_size, HEAD_DIM)
    )
    keys_rot = (
        rotate(keys_sum.reshape(TOK_DEV, kv_here, HEAD_DIM), own_pos)
        .astype(jnp.bfloat16)
        .reshape(TOK_DEV, key_cols)
    )
    values_bf = values_sum.astype(jnp.bfloat16)
    all_keys, all_values = (
        lax.all_gather(keys_rot, "dp", axis=0, tiled=True),
        lax.all_gather(values_bf, "dp", axis=0, tiled=True),
    )
    all_keys = all_keys.reshape(tokens_all, kv_here, HEAD_DIM)
    all_values = all_values.reshape(tokens_all, kv_here, HEAD_DIM)
    scores = jnp.einsum(
        "qkgh,skh->kgqs", query_rot, all_keys, preferred_element_type=jnp.float32
    ) * HEAD_DIM ** (-0.5)
    allowed = (own_doc[:, None] == key_doc[None, :]) & (key_index[None, :] <= own_index[:, None])
    exp_terms = jnp.where(allowed, jnp.exp(jnp.where(allowed, scores, 0.0)), 0.0)
    weights = (exp_terms / jnp.sum(exp_terms, -1, keepdims=True)).astype(jnp.bfloat16)
    head_mixed = (
        jnp.einsum("kgqs,skh->qkgh", weights, all_values, preferred_element_type=jnp.float32)
        .astype(jnp.bfloat16)
        .reshape(TOK_DEV, query_cols)
    )
    every_mixed = lax.all_gather(head_mixed, "dp", axis=0, tiled=True)
    partial_value = jnp.dot(every_mixed, w_output[0], preferred_element_type=jnp.float32)
    attn_sum = lax.psum_scatter(partial_value, "tp", scatter_dimension=0, tiled=True)
    target = lax.dynamic_slice_in_dim(moved_rows, lax.axis_index("tp") * TOK_DEV, TOK_DEV, 0)
    own_rows = (target.astype(jnp.float32) + attn_sum).astype(jnp.bfloat16)
    weight_grad, grad_enc, grad_dec = coder(own_rows, coder_weight.transpose(1, 0, 2), enc_bias, dec_bias)
    return (weight_grad.transpose(1, 0, 2), grad_enc.reshape(-1), grad_dec)


def solution(mesh):
    return jax.shard_map(
        shards,
        mesh=mesh,
        in_specs=(
            P("grp", "dp", None),
            P("grp", None),
            P("grp", "dp", "tp"),
            P("grp", "dp", "tp"),
            P("grp", "dp", "tp"),
            P("grp", "tp", "dp"),
            P(),
            P(("grp", "tp", "dp"), None, None),
            P(("grp", "tp", "dp")),
            P(),
        ),
        out_specs=(P(("grp", "tp", "dp"), None, None), P(("grp", "tp", "dp")), P()),
        check_vma=False,
    )
```

```python
import functools
import jax
import jax.numpy as jnp
import numpy as np
from jax import lax
from jax.experimental import pallas as pl
from jax.experimental.pallas import tpu as pltpu
from jax.sharding import PartitionSpec as P

HEAD_DIM = 128
TOK_DEV = 64
TOKENS = 512
BLOCK = 512
HALF = BLOCK // 2
RING = 4

sparsity = 1.0
rope_base = 500000.0

ROUTES = (
    ((0, 32, "xyz"), (32, 16, "yzx"), (48, 16, "zxy")),
    ((0, 32, "yzx"), (32, 16, "xyz"), (48, 16, "zxy")),
)


class Place:
    def __init__(self):
        self.m = lax.axis_index("grp")
        tp, dp = lax.axis_index("tp"), lax.axis_index("dp")
        self.tp, self.dp = tp, dp
        self.core = lax.rem(dp, 2)
        self.at = {"x": lax.div(dp, 2), "y": lax.div(tp, 2), "z": lax.rem(tp, 2) * 2 + self.m}

    def device(self, at, core):
        z = at["z"]
        return (lax.rem(z, 2), at["y"] * 2 + lax.div(z, 2), at["x"] * 2 + core)

    def beside(self, axis, step):
        return lax.rem(self.at[axis] + (step + RING), RING)

    def neighbour(self, axis, step):
        return self.device({**self.at, axis: self.beside(axis, step)}, self.core)

    def sibling(self):
        return self.device(self.at, 1 - self.core)

    def dp_peer(self, j):
        return (self.m, self.tp, lax.rem(self.dp + j, 8))

    def tp_peer(self, j):
        return (self.m, lax.rem(self.tp + j, 8), self.dp)

    def enter(self):
        barrier = pltpu.get_barrier_semaphore()
        peers = [self.dp_peer(j) for j in range(1, 8)] + [self.tp_peer(j) for j in range(1, 8)]
        for peer in peers + [self.neighbour("z", 1), self.neighbour("z", -1)]:
            pl.semaphore_signal(barrier, inc=1, device_id=peer, device_id_type=pl.DeviceIdType.MESH)
        pl.semaphore_wait(barrier, 16)


def part(buf, core, sel, rows, cols=(0, BLOCK)):
    index = [] if core is None else [core]
    z = sel.get("z")
    if z is None:
        index += [slice(None), slice(None)]
    elif isinstance(z, int):
        index += [z // 2, z % 2]
    else:
        index += [lax.div(z, 2), lax.rem(z, 2)]
    for axis in "yx":
        index.append(sel.get(axis, slice(None)))
    index += [pl.ds(*rows), pl.ds(*cols)]
    return buf.at[tuple(index)]


LOW, HIGH = (0, HALF), (HALF, HALF)


def send(src, dst, send_sem, recv_sem, device):
    copy = pltpu.make_async_remote_copy(
        src_ref=src, dst_ref=dst, send_sem=send_sem, recv_sem=recv_sem, device_id=device, device_id_type=pl.DeviceIdType.MESH
    )
    copy.start()
    return copy


def arrive(dst, sem, place):
    pltpu.make_async_remote_copy(
        src_ref=dst, dst_ref=dst, send_sem=sem, recv_sem=sem, device_id=place.sibling(), device_id_type=pl.DeviceIdType.MESH
    ).wait_recv()


def gather(place, core, buf, sems):
    send_sems, recv_sems, give_sems, take_sems = sems
    routes, other = ROUTES[core], ROUTES[1 - core]
    sibling = place.sibling()
    pending = []

    def sel_of(order, k, v):
        sel = {order[k]: v}
        for axis in order[k + 1 :]:
            sel[axis] = place.at[axis]
        return sel

    def give(i, j, sel, rows):
        ref = part(buf, core, sel, rows)
        pending.append(send(ref, ref, give_sems.at[i, j], take_sems.at[i, j], sibling))

    for i, (r0, n, order) in enumerate(routes):
        give(i, 9, dict(place.at), (r0, n))
    for k in range(3):
        for i, (r0, n, order) in enumerate(routes):
            ref = part(buf, core, sel_of(order, k, place.at[order[k]]), (r0, n))
            for j, step in enumerate((1, -1)):
                pending.append(send(ref, ref, send_sems.at[i, k, j], recv_sems.at[i, k, j], place.neighbour(order[k], step)))
        for i, (r0, n, order) in enumerate(routes):
            axis = order[k]
            for j, (step, cols) in enumerate(((1, LOW), (-1, HIGH))):
                sel = sel_of(order, k, place.beside(axis, -step))
                arrive(part(buf, core, sel, (r0, n)), recv_sems.at[i, k, j], place)
                ref = part(buf, core, sel, (r0, n), cols)
                pending.append(send(ref, ref, send_sems.at[i, k, 2 + j], recv_sems.at[i, k, 2 + j], place.neighbour(axis, step)))
                give(i, k * 3 + j, sel, (r0, n))
        for i, (r0, n, order) in enumerate(routes):
            sel = sel_of(order, k, place.beside(order[k], 2))
            for j, cols in enumerate((LOW, HIGH)):
                arrive(part(buf, core, sel, (r0, n), cols), recv_sems.at[i, k, 2 + j], place)
            give(i, k * 3 + 2, sel, (r0, n))
    for i, (r0, n, order) in enumerate(other):
        for k in range(3):
            for j, v in enumerate((-1, 1, 2)):
                arrive(part(buf, 1 - core, sel_of(order, k, place.beside(order[k], v)), (r0, n)), take_sems.at[i, k * 3 + j], place)
        arrive(part(buf, 1 - core, dict(place.at), (r0, n)), take_sems.at[i, 9], place)
    for copy in pending:
        copy.wait_send()


def spread(sel, i):
    at, rest = {}, i
    for axis in "xyz":
        if sel.get(axis) is None:
            at[axis] = lax.rem(rest, RING)
            rest = lax.div(rest, RING)
        else:
            at[axis] = sel[axis]
    z = at["z"]
    zh, zl = (z // 2, z % 2) if isinstance(z, int) else (lax.div(z, 2), lax.rem(z, 2))
    return zh, zl, at["y"], at["x"]


def scatter_sum(place, core, sums, landing, result, sems):
    send_sems, recv_sems = sems
    routes = ROUTES[core]
    pending = []

    def sel_of(order, k, v, done):
        sel = {order[k]: v}
        for axis in order[:k]:
            sel[axis] = done if done is not None else place.at[axis]
        return sel

    def add(order, k, target, slots, rows, cols, into_result):
        sel = sel_of(order, k, target, None)
        count = RING ** (2 - k)

        def step(i, carry):
            own = spread(sel, i)
            window = (pl.ds(*rows), pl.ds(*cols))
            total = sums[own + window].astype(jnp.float32)
            for slot in slots:
                total = total + landing[spread(sel_of(order, k, slot, 3), i) + window].astype(jnp.float32)
            if into_result:
                result[window] = total
            else:
                sums[own + window] = total.astype(jnp.bfloat16)
            return carry

        lax.fori_loop(0, count, step, 0)

    for k in range(3):
        for i, (r0, n, order) in enumerate(routes):
            axis = order[k]
            for j, (step, slot, v, cols) in enumerate(((1, 0, 2, LOW), (-1, 0, 2, HIGH), (1, 1, 1, HIGH), (-1, 2, -1, LOW))):
                src = part(sums, None, sel_of(order, k, place.beside(axis, v), None), (r0, n), cols)
                dst = part(landing, None, sel_of(order, k, slot, 3), (r0, n), cols)
                pending.append(send(src, dst, send_sems.at[i, k, j], recv_sems.at[i, k, j], place.neighbour(axis, step)))
        for i, (r0, n, order) in enumerate(routes):
            axis = order[k]
            for j, (step, slot, cols) in enumerate(((1, 1, LOW), (-1, 2, HIGH))):
                arrive(part(landing, None, sel_of(order, k, 0, 3), (r0, n), cols), recv_sems.at[i, k, j], place)
                add(order, k, place.beside(axis, step), (0,), (r0, n), cols, False)
                src = part(sums, None, sel_of(order, k, place.beside(axis, step), None), (r0, n), cols)
                dst = part(landing, None, sel_of(order, k, slot, 3), (r0, n), cols)
                pending.append(send(src, dst, send_sems.at[i, k, 4 + j], recv_sems.at[i, k, 4 + j], place.neighbour(axis, step)))
        for i, (r0, n, order) in enumerate(routes):
            for j, (slot, cols) in ((2, (1, HIGH)), (3, (2, LOW)), (4, (1, LOW)), (5, (2, HIGH))):
                arrive(part(landing, None, sel_of(order, k, slot, 3), (r0, n), cols), recv_sems.at[i, k, j], place)
            add(order, k, place.at[order[k]], (1, 2), (r0, n), (0, BLOCK), k == 2)
    for copy in pending:
        copy.wait_send()


def gelu_pair(pre_act):
    normal_cdf = 0.5 * (1.0 + lax.erf(pre_act * 0.7071067811865476))
    density = jnp.exp(-0.5 * pre_act * pre_act) * 0.3989422804014327
    return (pre_act * normal_cdf, normal_cdf + pre_act * density)


def nt(a, b):
    return lax.dot_general(a, b, (((1,), (1,)), ((), ())), preferred_element_type=jnp.float32)


def nn(a, b):
    return lax.dot_general(a, b, (((1,), (0,)), ((), ())), preferred_element_type=jnp.float32)


def chunk_of(k):
    mm, x, c = lax.div(k, 8), lax.rem(lax.div(k, 2), RING), lax.rem(k, 2)
    return mm, x, c, pl.ds(pl.multiple_of((x * 2 + c) * BLOCK, BLOCK), BLOCK)


def token_rows(buf, mm, x, c):
    return buf[c, :, mm, :, x].reshape(TOKENS, BLOCK)


def doc_layout(lengths, token_index):
    doc, start, end = jnp.zeros_like(token_index), jnp.zeros_like(token_index), 0
    for i in range(4):
        end = end + lengths[i]
        passed = (token_index >= end).astype(jnp.int32)
        doc, start = doc + passed, start + passed * lengths[i]
    return doc, token_index - start


def attend_layer(place, refs, bufs, sems, work):
    res, gain, w_query, w_key, w_value, w_output, lengths, freq = refs
    nsend, moved, raw, pair_out, pair_in, own_sum, qkv_out, qkv_in, kv, mixed, part_f, part_out, part_in = bufs
    moved_s, moved_r, raw_s, raw_r, pair_s, pair_r, qkv_s, qkv_r, kv_s, kv_r, mixed_s, mixed_r, part_s, part_r = sems
    dp, tp, core, x = place.dp, place.tp, place.core, place.at["x"]
    pending = []

    for r in range(0, TOK_DEV, 16):
        wide = res[r : r + 16, :].astype(jnp.float32)
        scale = lax.rsqrt(jnp.mean(wide * wide, -1, keepdims=True) + 1e-05)
        normed = (wide * scale * gain[...].astype(jnp.float32)).astype(jnp.bfloat16)
        for d in range(8):
            nsend[d, r : r + 16, :] = normed[:, d * BLOCK : (d + 1) * BLOCK]
    place.enter()
    for j in range(1, 8):
        there = lax.rem(dp + j, 8)
        pending.append(send(nsend.at[there], moved.at[core, x], moved_s.at[j], moved_r.at[j], place.dp_peer(j)))
    moved[core, x] = nsend[dp]

    def columns(d):
        return pl.ds(pl.multiple_of(d * BLOCK, BLOCK), BLOCK)

    @pl.when(dp == tp)
    def _():
        for j in range(1, 8):
            send(res.at[:, columns(lax.rem(dp + j, 8))], raw, raw_s.at[j], raw_r, place.dp_peer(j))
        raw[...] = res[:, columns(dp)]

    here = dp * TOK_DEV + lax.broadcasted_iota(jnp.int32, (TOK_DEV, 1), 0)
    keys_at = lax.broadcasted_iota(jnp.int32, (1, TOKENS), 1)
    doc, pos = doc_layout(lengths, here)
    key_doc, _ = doc_layout(lengths, keys_at)
    angles = pos.astype(jnp.float32) * freq[...]
    lane = lax.broadcasted_iota(jnp.int32, (1, HEAD_DIM), 1)
    cosine = jnp.cos(angles)
    sine = jnp.sin(angles) * jnp.where(lane < HEAD_DIM // 2, -1.0, 1.0)
    allowed = (doc == key_doc) & (keys_at <= here)
    work(2)

    for j in range(1, 8):
        src = lax.rem(dp + 8 - j, 8)
        arrive(moved.at[lax.rem(src, 2), lax.div(src, 2)], moved_r.at[j], place)

    def project(c, out):
        rows_in = moved[c].reshape(RING * TOK_DEV, BLOCK)
        for w_ref, at, width in ((w_query, 0, 512), (w_key, 512, 128), (w_value, 640, 128)):
            out[:, :, at : at + width] = nn(rows_in, w_ref[...]).reshape(RING, TOK_DEV, width)

    project(1 - core, pair_out)
    pair = send(pair_out, pair_in, pair_s, pair_r, place.sibling())
    project(core, own_sum)
    pair.wait_recv()
    own_sum[...] = own_sum[...] + pair_in[...]
    qkv_out[...] = own_sum[...].astype(jnp.bfloat16)
    for j in range(1, RING):
        there = lax.rem(x + j, RING)
        pending.append(send(qkv_out.at[there], qkv_in.at[j], qkv_s.at[j], qkv_r.at[j], place.dp_peer(2 * j)))
    work(2)
    summed = own_sum[x]
    for j in range(1, RING):
        arrive(qkv_in.at[j], qkv_r.at[j], place)
        summed = summed + qkv_in[j].astype(jnp.float32)

    def rotate(values):
        return (values * cosine + pltpu.roll(values, HEAD_DIM // 2, 1) * sine).astype(jnp.bfloat16)

    kv[dp, :, :HEAD_DIM] = rotate(summed[:, 512:640])
    kv[dp, :, HEAD_DIM:] = summed[:, 640:].astype(jnp.bfloat16)
    for j in range(1, 8):
        pending.append(send(kv.at[dp], kv.at[dp], kv_s.at[j], kv_r.at[j], place.dp_peer(j)))
    query = jnp.concatenate([rotate(summed[:, h * HEAD_DIM : (h + 1) * HEAD_DIM]) for h in range(4)], 0)
    work(1)
    for j in range(1, 8):
        arrive(kv.at[lax.rem(dp + 8 - j, 8)], kv_r.at[j], place)

    all_kv = kv[...].reshape(TOKENS, 2 * HEAD_DIM)
    scores = nt(query, all_kv[:, :HEAD_DIM]) * HEAD_DIM ** (-0.5)
    mask = jnp.concatenate([allowed] * 4, 0)
    terms = jnp.where(mask, jnp.exp(jnp.where(mask, scores, 0.0)), 0.0)
    weights = (terms / jnp.sum(terms, -1, keepdims=True)).astype(jnp.bfloat16)
    heads = nn(weights, all_kv[:, HEAD_DIM:]).astype(jnp.bfloat16)
    for h in range(4):
        mixed[dp, :, h * HEAD_DIM : (h + 1) * HEAD_DIM] = heads[h * TOK_DEV : (h + 1) * TOK_DEV]
    for j in range(1, 8):
        pending.append(send(mixed.at[dp], mixed.at[dp], mixed_s.at[j], mixed_r.at[j], place.dp_peer(j)))
    work(2)
    for j in range(1, 8):
        arrive(mixed.at[lax.rem(dp + 8 - j, 8)], mixed_r.at[j], place)

    outs = nn(mixed[...].reshape(TOKENS, BLOCK), w_output[...]).reshape(8, TOK_DEV, BLOCK)
    part_f[...] = outs
    part_out[...] = outs.astype(jnp.bfloat16)
    for j in range(1, 8):
        there = lax.rem(tp + j, 8)
        pending.append(send(part_out.at[there], part_in.at[j], part_s.at[j], part_r.at[j], place.tp_peer(j)))
    work(1)

    @pl.when(dp != tp)
    def _():
        arrive(raw, raw_r, place)

    total = part_f[tp]
    for j in range(1, 8):
        arrive(part_in.at[j], part_r.at[j], place)
        total = total + part_in[j].astype(jnp.float32)

    @pl.when(dp == tp)
    def _():
        for j in range(1, 8):
            pltpu.make_async_remote_copy(
                src_ref=res.at[:, columns(lax.rem(dp + j, 8))], dst_ref=raw, send_sem=raw_s.at[j], recv_sem=raw_r,
                device_id=place.dp_peer(j), device_id_type=pl.DeviceIdType.MESH,
            ).wait_send()

    pair.wait_send()
    for copy in pending:
        copy.wait_send()
    return (raw[...].astype(jnp.float32) + total).astype(jnp.bfloat16)


def column_of(row):
    return jnp.broadcast_to(row, (128, 128)).T[:, :1]


def row_of(column):
    return jnp.broadcast_to(column, (128, 128)).T[:1]


SPLIT = 64


def step_kernel(
    res, gain, w_query, w_key, w_value, w_output, lengths, freq, w_hbm, enc_ref, dec_ref,
    rows_hbm, errs_hbm, w_out, act_t, pre_t, scale_ref, genc_ref,
    nsend, moved, raw, pair_out, pair_in, own_sum, qkv_out, qkv_in, kv, mixed, part_f, part_out, part_in,
    own_ref, rows, errs, w_raw, w, sums, give, taken, landing, result, total, act, slope, norms, latsum,
    moved_s, moved_r, raw_s, raw_r, pair_s, pair_r, qkv_s, qkv_r, kv_s, kv_r, mixed_s, mixed_r, part_s, part_r,
    w_sem, rows_send, rows_recv, rows_give, rows_take, errs_send, errs_recv, errs_give, errs_take,
    sum_send, sum_recv, pair_send, pair_recv, out_sem,
):
    place = Place()
    m, core = place.m, place.core
    loads = [
        pltpu.make_async_copy(w_hbm.at[pl.ds(i * SPLIT, SPLIT)], w_raw.at[i % 2], w_sem.at[i % 2])
        for i in range(BLOCK // SPLIT)
    ]
    loads[0].start()
    loads[1].start()
    done = [0]

    def work(count):
        for i in range(done[0], done[0] + count):
            at = pl.ds(i * SPLIT, SPLIT)
            loads[i].wait()

            def step(k, carry):
                cols = pl.ds(pl.multiple_of(k * BLOCK, BLOCK), BLOCK)
                for mm in (0, 1):
                    w[mm, at, cols] = w_raw[i % 2, :, mm, cols]
                return carry

            lax.fori_loop(0, 8, step, 0)
            if i + 2 < len(loads):
                loads[i + 2].start()
        done[0] += count

    layer_bufs = (nsend, moved, raw, pair_out, pair_in, own_sum, qkv_out, qkv_in, kv, mixed, part_f, part_out, part_in)
    layer_sems = (moved_s, moved_r, raw_s, raw_r, pair_s, pair_r, qkv_s, qkv_r, kv_s, kv_r, mixed_s, mixed_r, part_s, part_r)
    layer_refs = (res, gain, w_query, w_key, w_value, w_output, lengths, freq)
    own_ref[...] = attend_layer(place, layer_refs, layer_bufs, layer_sems, work)
    outs = [pltpu.make_async_copy(w, w_out, out_sem.at[0])]
    outs[0].start()
    own = (lax.div(place.at["z"], 2), m, place.at["y"], place.at["x"])
    rows[(core,) + own] = own_ref[...]
    for c in (0, 1):
        pl.when(core == c)(functools.partial(gather, place, c, rows, (rows_send, rows_recv, rows_give, rows_take)))
    outs.append(pltpu.make_async_copy(rows, rows_hbm, out_sem.at[1]))
    outs[1].start()

    def norm_step(i, carry):
        at = pl.ds(pl.multiple_of(i * 16, 16), 16)
        for mm in (0, 1):
            wide = w[mm, at, :].astype(jnp.float32)
            norms[mm, at, :] = jnp.sqrt(jnp.sum(wide * wide, -1, keepdims=True) + 1e-06)
        return carry

    lax.fori_loop(0, TOKENS // 16, norm_step, 0)

    def contract(buf):
        total[...] = jnp.zeros_like(total)

        def step(k, carry):
            mm, x, c, cols = chunk_of(k)
            total[...] += nt(w[mm, :, cols], token_rows(buf, mm, x, c))
            return carry

        lax.fori_loop(0, 16, step, 0)

    contract(rows)
    for i in range(4):
        at = pl.ds(i * 128, 128)
        lat, slope[at, :] = gelu_pair(total[at, :] + column_of(enc_ref[i : i + 1, :]))
        latsum[at, :] = jnp.sum(lat, -1, keepdims=True)
        act_t[at, :] = lat.astype(jnp.bfloat16)
        act[:, at] = lat.T.astype(jnp.bfloat16)

    pairs = []
    for k in range(8):
        mm, x = k // 4, k % 4
        cols = pl.ds(pl.multiple_of((x * 2 + 1 - core) * BLOCK, BLOCK), BLOCK)
        give[:, mm, :, x] = nn(act[...], w[mm, :, cols]).astype(jnp.bfloat16).reshape(2, RING, TOK_DEV, BLOCK)
        pairs.append(send(give.at[:, mm, :, x], taken.at[:, mm, :, x], pair_send.at[k], pair_recv.at[k], place.sibling()))
    for k in range(8):
        mm, x = k // 4, k % 4
        cols = pl.ds(pl.multiple_of((x * 2 + core) * BLOCK, BLOCK), BLOCK)
        here = nn(act[...], w[mm, :, cols])
        pairs[k].wait_recv()
        there = taken[:, mm, :, x].reshape(TOKENS, BLOCK).astype(jnp.float32)
        sums[:, mm, :, x] = (here + there).astype(jnp.bfloat16).reshape(2, RING, TOK_DEV, BLOCK)
    for copy in pairs:
        copy.wait_send()
    for c in (0, 1):
        pl.when(core == c)(functools.partial(scatter_sum, place, c, sums, landing, result, (sum_send, sum_recv)))
    bias = dec_ref[pl.ds(m * 8 + place.dp, 1), :]
    errs[(core,) + own] = (result[...] + bias - own_ref[...].astype(jnp.float32)).astype(jnp.bfloat16)
    for c in (0, 1):
        pl.when(core == c)(functools.partial(gather, place, c, errs, (errs_send, errs_recv, errs_give, errs_take)))
    outs.append(pltpu.make_async_copy(errs, errs_hbm, out_sem.at[2]))
    outs[2].start()

    contract(errs)
    for i in range(4):
        at = pl.ds(i * 128, 128)
        norm_total = norms[0, at, :] + norms[1, at, :]
        pre_grad = (2.0 / TOKENS * total[at, :] + sparsity / TOKENS * norm_total) * slope[at, :]
        genc_ref[i : i + 1, :] = row_of(jnp.sum(pre_grad, -1, keepdims=True))
        pre_t[at, :] = pre_grad.astype(jnp.bfloat16)
    scale_ref[...] = sparsity / TOKENS * latsum[...] / norms[...]
    for copy in outs:
        copy.wait()


def grad_kernel(rows, errs, w, act_t, pre_t, scale, genc, gw, genc_out, gdec):
    for mm in (0, 1):
        err = errs[0, :, mm, :, 0].reshape(TOKENS, BLOCK)
        grad = 2.0 / TOKENS * nn(act_t[...], err) + nn(pre_t[...], rows[0, :, mm, :, 0].reshape(TOKENS, BLOCK))
        gw[:, mm, :] = (grad + scale[mm] * w[mm].astype(jnp.float32)).astype(jnp.bfloat16)
        ones = jnp.ones((16, TOKENS), jnp.bfloat16)
        gdec[mm : mm + 1, :] = 2.0 / TOKENS * nn(ones, err)[:1]
    genc_out[...] = genc[...]


def shards(
    residual, norm_gain, w_query, w_key, w_value, w_output, doc_lengths, coder_weight, enc_bias, dec_bias
):
    latents, _, features = coder_weight.shape
    blocks = (2, 2, RING, RING, TOK_DEV, BLOCK)
    bf16, f32 = jnp.bfloat16, jnp.float32
    dma, vm = pltpu.SemaphoreType.DMA, pltpu.VMEM
    vmem = pl.BlockSpec(memory_space=pltpu.VMEM)
    hbm = pl.BlockSpec(memory_space=pl.ANY)
    ring = [dma((3, 3, 4)), dma((3, 3, 4)), dma((3, 10)), dma((3, 10))]
    half = np.arange(HEAD_DIM // 2)
    freq = np.concatenate([rope_base ** (-half * 2.0 / HEAD_DIM)] * 2)[None].astype(np.float32)
    block = (TOK_DEV, BLOCK)
    rows, errs, w_t, act_t, pre_t, scale, genc = pl.pallas_call(
        step_kernel,
        out_shape=(
            jax.ShapeDtypeStruct((2,) + blocks, bf16),
            jax.ShapeDtypeStruct((2,) + blocks, bf16),
            jax.ShapeDtypeStruct((2, latents, features), bf16),
            jax.ShapeDtypeStruct((latents, TOKENS), bf16),
            jax.ShapeDtypeStruct((latents, TOKENS), bf16),
            jax.ShapeDtypeStruct((2, latents, 1), f32),
            jax.ShapeDtypeStruct((4, 128), f32),
        ),
        in_specs=[vmem] * 6 + [pl.BlockSpec(memory_space=pltpu.SMEM), vmem, hbm, vmem, vmem],
        out_specs=(hbm, hbm, hbm, vmem, vmem, vmem, vmem),
        scratch_shapes=[
            vm((8,) + block, bf16),
            vm((2, RING) + block, bf16),
            vm(block, bf16),
            vm((RING, TOK_DEV, 768), f32),
            vm((RING, TOK_DEV, 768), f32),
            vm((RING, TOK_DEV, 768), f32),
            vm((RING, TOK_DEV, 768), bf16),
            vm((RING, TOK_DEV, 768), bf16),
            vm((8, TOK_DEV, 2 * HEAD_DIM), bf16),
            vm((8,) + block, bf16),
            vm((8,) + block, f32),
            vm((8,) + block, bf16),
            vm((8,) + block, bf16),
            vm(block, bf16),
            vm((2,) + blocks, bf16),
            vm((2,) + blocks, bf16),
            vm((2, SPLIT, 2, features), bf16),
            vm((2, latents, features), bf16),
            vm(blocks, bf16),
            vm(blocks, bf16),
            vm(blocks, bf16),
            vm(blocks, bf16),
            vm(block, f32),
            vm((latents, TOKENS), f32),
            vm((TOKENS, latents), bf16),
            vm((latents, TOKENS), f32),
            vm((2, latents, 1), f32),
            vm((latents, 1), f32),
            *[dma((8,)), dma((8,)), dma((8,)), dma(()), dma(()), dma(())],
            *[dma((8,)) for _ in range(8)],
            dma((2,)),
            *ring,
            *ring,
            dma((3, 3, 6)),
            dma((3, 3, 6)),
            dma((8,)),
            dma((8,)),
            dma((3,)),
        ],
        compiler_params=pltpu.CompilerParams(collective_id=0, has_side_effects=True, vmem_limit_bytes=62 * 1024 * 1024),
        cost_estimate=pl.CostEstimate(flops=6 * TOKENS * latents * 2 * features, bytes_accessed=40 << 20, transcendentals=0),
    )(
        residual[0], norm_gain, w_query[0], w_key[0], w_value[0], w_output[0], doc_lengths, jnp.asarray(freq),
        coder_weight, enc_bias.reshape(4, 128), dec_bias.reshape(16, BLOCK),
    )
    set_spec = pl.BlockSpec((1, 2, 2, RING, 1) + block, lambda k: (lax.rem(k, 2), 0, 0, 0, lax.div(k, 2), 0, 0))
    whole = lambda *shape: pl.BlockSpec(shape, lambda k: (0,) * len(shape))
    weight_grad, grad_enc, grad_dec = pl.pallas_call(
        grad_kernel,
        grid=(8,),
        out_shape=(
            jax.ShapeDtypeStruct((latents, 2, features), bf16),
            jax.ShapeDtypeStruct((4, 128), f32),
            jax.ShapeDtypeStruct((2, features), f32),
        ),
        in_specs=[
            set_spec,
            set_spec,
            pl.BlockSpec((2, latents, BLOCK), lambda k: (0, 0, k)),
            whole(latents, TOKENS),
            whole(latents, TOKENS),
            whole(2, latents, 1),
            whole(4, 128),
        ],
        out_specs=(
            pl.BlockSpec((latents, 2, BLOCK), lambda k: (0, 0, k)),
            whole(4, 128),
            pl.BlockSpec((2, BLOCK), lambda k: (0, k)),
        ),
        compiler_params=pltpu.CompilerParams(vmem_limit_bytes=48 * 1024 * 1024),
    )(rows, errs, w_t, act_t, pre_t, scale, genc)
    return (weight_grad, grad_enc.reshape(-1), grad_dec)


def solution(mesh):
    return jax.shard_map(
        shards,
        mesh=mesh,
        in_specs=(
            P("grp", "dp", None),
            P("grp", None),
            P("grp", "dp", "tp"),
            P("grp", "dp", "tp"),
            P("grp", "dp", "tp"),
            P("grp", "tp", "dp"),
            P(),
            P(("grp", "tp", "dp"), None, None),
            P(("grp", "tp", "dp")),
            P(),
        ),
        out_specs=(P(("grp", "tp", "dp"), None, None), P(("grp", "tp", "dp")), P()),
        check_vma=False,
    )
```

```python
import functools
import jax
import jax.numpy as jnp
import numpy as np
from jax import lax
from jax.experimental import pallas as pl
from jax.experimental.pallas import tpu as pltpu
from jax.sharding import PartitionSpec as P

HEAD_DIM = 128
TOK_DEV = 64
TOKENS = 512
BLOCK = 512
RING = 4
HALF = TOK_DEV // 2
HALF_TOKENS = TOKENS // 2

sparsity = 1.0
rope_base = 500000.0

ROUTES = (((0, 16), (0, 384), "xyz"), ((16, 16), (0, 384), "yzx"), ((0, 32), (384, 128), "zxy"))


class Place:
    def __init__(self):
        self.m = lax.axis_index("grp")
        tp, dp = lax.axis_index("tp"), lax.axis_index("dp")
        self.tp, self.dp = tp, dp
        self.core = lax.rem(dp, 2)
        self.at = {"x": lax.div(dp, 2), "y": lax.div(tp, 2), "z": lax.rem(tp, 2) * 2 + self.m}

    def device(self, at, core):
        z = at["z"]
        return (lax.rem(z, 2), at["y"] * 2 + lax.div(z, 2), at["x"] * 2 + core)

    def beside(self, axis, step):
        return lax.rem(self.at[axis] + (step + RING), RING)

    def neighbour(self, axis, step):
        return self.device({**self.at, axis: self.beside(axis, step)}, self.core)

    def sibling(self):
        return self.device(self.at, 1 - self.core)

    def dp_peer(self, j):
        return (self.m, self.tp, lax.rem(self.dp + j, 8))

    def tp_peer(self, j):
        return (self.m, lax.rem(self.tp + j, 8), self.dp)

    def enter(self):
        barrier = pltpu.get_barrier_semaphore()
        peers = [self.dp_peer(j) for j in range(1, 8)] + [self.tp_peer(j) for j in range(1, 8)]
        for peer in peers + [self.neighbour("z", 1), self.neighbour("z", -1)]:
            pl.semaphore_signal(barrier, inc=1, device_id=peer, device_id_type=pl.DeviceIdType.MESH)
        pl.semaphore_wait(barrier, 16)


def part(buf, lead, sel, rows, cols):
    z = sel.get("z")
    if z is None:
        index = [slice(None), slice(None)]
    elif isinstance(z, int):
        index = [z // 2, z % 2]
    else:
        index = [lax.div(z, 2), lax.rem(z, 2)]
    index += [sel.get(axis, slice(None)) for axis in "yx"]
    return buf.at[tuple(lead) + tuple(index) + (pl.ds(*rows), pl.ds(*cols))]


def send(src, dst, send_sem, recv_sem, device):
    copy = pltpu.make_async_remote_copy(
        src_ref=src, dst_ref=dst, send_sem=send_sem, recv_sem=recv_sem, device_id=device, device_id_type=pl.DeviceIdType.MESH
    )
    copy.start()
    return copy


def arrive(dst, sem, place):
    pltpu.make_async_remote_copy(
        src_ref=dst, dst_ref=dst, send_sem=sem, recv_sem=sem, device_id=place.sibling(), device_id_type=pl.DeviceIdType.MESH
    ).wait_recv()


def gather(place, h, buf, sems, pending):
    send_sems, recv_sems, give_sems, take_sems = sems
    mine, other = (place.core, h), (1 - place.core, h)

    def sel_of(order, k, v):
        return {order[k]: v, **{axis: place.at[axis] for axis in order[k + 1 :]}}

    def give(j):
        for rows, cols, order in ROUTES:
            ref = part(buf, mine, sel_of(order, 2, place.beside(order[2], -j)), rows, cols)
            send(ref, ref, give_sems.at[h], take_sems.at[h], place.sibling())

    one_ring = [buf.at[mine + (0,) * (4 - k)] for k in (0, 1, 2)]
    three_rings = [buf.at[mine + (0, 0, 0, pl.ds(0, 3))], buf.at[mine + (0, 0, pl.ds(0, 3))], buf.at[mine + (slice(None), slice(None), pl.ds(0, 3))]]
    for k in range(3):
        for j in range(1, RING):
            for rows, cols, order in ROUTES:
                ref = part(buf, mine, sel_of(order, k, place.at[order[k]]), rows, cols)
                send(ref, ref, send_sems.at[h, k], recv_sems.at[h, k, j], place.neighbour(order[k], j))
        pending.append((three_rings[k], send_sems.at[h, k]))
        if k == 2:
            give(0)
        yield
        for j in range(1, RING):
            arrive(one_ring[k], recv_sems.at[h, k, j], place)
            if k == 2:
                give(j)
    pending.append((buf.at[mine], give_sems.at[h]))
    yield
    arrive(buf.at[other], take_sems.at[h], place)


def spread(sel, i):
    at, rest = {}, i
    for axis in "xyz":
        if sel.get(axis) is None:
            at[axis] = lax.rem(rest, RING)
            rest = lax.div(rest, RING)
        else:
            at[axis] = sel[axis]
    z = at["z"]
    zh, zl = (z // 2, z % 2) if isinstance(z, int) else (lax.div(z, 2), lax.rem(z, 2))
    return zh, zl, at["y"], at["x"]


def scatter_sum(place, h, sums, landing, result, sems, pending):
    send_sems, recv_sems = sems

    def sel_of(order, k, v, done):
        return {order[k]: v, **{axis: place.at[axis] if done is None else done for axis in order[:k]}}

    def add(order, k, rows, cols):
        window = (pl.ds(*rows), pl.ds(*cols))

        def step(i, carry):
            own = (h,) + spread(sel_of(order, k, place.at[order[k]], None), i) + window
            total = sums[own].astype(jnp.float32)
            for j in range(1, RING):
                total = total + landing[(h,) + spread(sel_of(order, k, j, 0), i) + window].astype(jnp.float32)
            if k == 2:
                result[(h,) + window] = total
            else:
                sums[own] = total.astype(jnp.bfloat16)
            return carry

        lax.fori_loop(0, RING ** (2 - k), step, 0)

    three_rings = [landing.at[h, :, :, pl.ds(0, 3)], landing.at[h, 0, 0, pl.ds(0, 3)], landing.at[h, 0, 0, 0, pl.ds(0, 3)]]
    for k in range(3):
        for j in range(1, RING):
            for rows, cols, order in ROUTES:
                src = part(sums, (h,), sel_of(order, k, place.beside(order[k], j), None), rows, cols)
                dst = part(landing, (h,), sel_of(order, k, j, 0), rows, cols)
                send(src, dst, send_sems.at[h, k], recv_sems.at[h, k], place.neighbour(order[k], j))
        pending.append((three_rings[k], send_sems.at[h, k]))
        yield
        arrive(three_rings[k], recv_sems.at[h, k], place)
        for rows, cols, order in ROUTES:
            add(order, k, rows, cols)


def gelu_pair(pre_act):
    normal_cdf = 0.5 * (1.0 + lax.erf(pre_act * 0.7071067811865476))
    density = jnp.exp(-0.5 * pre_act * pre_act) * 0.3989422804014327
    return (pre_act * normal_cdf, normal_cdf + pre_act * density)


def nt(a, b):
    return lax.dot_general(a, b, (((1,), (1,)), ((), ())), preferred_element_type=jnp.float32)


def nn(a, b):
    return lax.dot_general(a, b, (((1,), (0,)), ((), ())), preferred_element_type=jnp.float32)


def chunk_of(k):
    mm, x, c = lax.div(k, 8), lax.rem(lax.div(k, 2), RING), lax.rem(k, 2)
    return mm, x, c, pl.ds(pl.multiple_of((x * 2 + c) * BLOCK, BLOCK), BLOCK)


def token_rows(buf, h, mm, x, c):
    return buf[c, h, :, mm, :, x].reshape(HALF_TOKENS, BLOCK)


def doc_layout(lengths, token_index):
    doc, start, end = jnp.zeros_like(token_index), jnp.zeros_like(token_index), 0
    for i in range(4):
        end = end + lengths[i]
        passed = (token_index >= end).astype(jnp.int32)
        doc, start = doc + passed, start + passed * lengths[i]
    return doc, token_index - start


def attend_layer(place, refs, bufs, sems, work):
    res, gain, w_query, w_key, w_value, w_output, lengths, freq = refs
    nsend, moved, raw, pair_out, pair_in, own_sum, qkv_out, qkv_in, kv, mixed, part_f, part_out, part_in = bufs
    moved_s, moved_r, raw_s, raw_r, pair_s, pair_r, qkv_s, qkv_r, kv_s, kv_r, mixed_s, mixed_r, part_s, part_r = sems
    dp, tp, core, x = place.dp, place.tp, place.core, place.at["x"]
    pending = []

    for r in range(0, TOK_DEV, 16):
        wide = res[r : r + 16, :].astype(jnp.float32)
        scale = lax.rsqrt(jnp.mean(wide * wide, -1, keepdims=True) + 1e-05)
        normed = (wide * scale * gain[...].astype(jnp.float32)).astype(jnp.bfloat16)
        for d in range(8):
            nsend[d, r : r + 16, :] = normed[:, d * BLOCK : (d + 1) * BLOCK]
    place.enter()
    for j in range(1, 8):
        there = lax.rem(dp + j, 8)
        send(nsend.at[there], moved.at[core, x], moved_s, moved_r, place.dp_peer(j))
    pending.append((nsend.at[pl.ds(0, 7)], moved_s))
    moved[core, x] = nsend[dp]

    def columns(d):
        return pl.ds(pl.multiple_of(d * BLOCK, BLOCK), BLOCK)

    @pl.when(dp == tp)
    def _():
        for j in range(1, 8):
            send(res.at[:, columns(lax.rem(dp + j, 8))], raw, raw_s.at[j], raw_r, place.dp_peer(j))
        raw[...] = res[:, columns(dp)]

    here = dp * TOK_DEV + lax.broadcasted_iota(jnp.int32, (TOK_DEV, 1), 0)
    keys_at = lax.broadcasted_iota(jnp.int32, (1, TOKENS), 1)
    doc, pos = doc_layout(lengths, here)
    key_doc, _ = doc_layout(lengths, keys_at)
    angles = pos.astype(jnp.float32) * freq[...]
    lane = lax.broadcasted_iota(jnp.int32, (1, HEAD_DIM), 1)
    cosine = jnp.cos(angles)
    sine = jnp.sin(angles) * jnp.where(lane < HEAD_DIM // 2, -1.0, 1.0)
    allowed = (doc == key_doc) & (keys_at <= here)
    work(2)

    arrive(nsend.at[pl.ds(0, 7)], moved_r, place)

    def project(c, out):
        rows_in = moved[c].reshape(RING * TOK_DEV, BLOCK)
        for w_ref, at, width in ((w_query, 0, 512), (w_key, 512, 128), (w_value, 640, 128)):
            out[:, :, at : at + width] = nn(rows_in, w_ref[...]).reshape(RING, TOK_DEV, width)

    project(1 - core, pair_out)
    pair = send(pair_out, pair_in, pair_s, pair_r, place.sibling())
    project(core, own_sum)
    pair.wait_recv()
    own_sum[...] = own_sum[...] + pair_in[...]
    qkv_out[...] = own_sum[...].astype(jnp.bfloat16)
    for j in range(1, RING):
        there = lax.rem(x + j, RING)
        send(qkv_out.at[there], qkv_in.at[j], qkv_s, qkv_r, place.dp_peer(2 * j))
    pending.append((qkv_out.at[pl.ds(1, 3)], qkv_s))
    work(2)
    summed = own_sum[x]
    arrive(qkv_in.at[pl.ds(1, 3)], qkv_r, place)
    for j in range(1, RING):
        summed = summed + qkv_in[j].astype(jnp.float32)

    def rotate(values):
        return (values * cosine + pltpu.roll(values, HEAD_DIM // 2, 1) * sine).astype(jnp.bfloat16)

    kv[dp, :, :HEAD_DIM] = rotate(summed[:, 512:640])
    kv[dp, :, HEAD_DIM:] = summed[:, 640:].astype(jnp.bfloat16)
    for j in range(1, 8):
        send(kv.at[dp], kv.at[dp], kv_s, kv_r, place.dp_peer(j))
    pending.append((kv.at[pl.ds(0, 7)], kv_s))
    query = jnp.concatenate([rotate(summed[:, h * HEAD_DIM : (h + 1) * HEAD_DIM]) for h in range(4)], 0)
    work(1)
    arrive(kv.at[pl.ds(0, 7)], kv_r, place)

    all_kv = kv[...].reshape(TOKENS, 2 * HEAD_DIM)
    scores = nt(query, all_kv[:, :HEAD_DIM]) * HEAD_DIM ** (-0.5)
    mask = jnp.concatenate([allowed] * 4, 0)
    terms = jnp.where(mask, jnp.exp(jnp.where(mask, scores, 0.0)), 0.0)
    weights = (terms / jnp.sum(terms, -1, keepdims=True)).astype(jnp.bfloat16)
    heads = nn(weights, all_kv[:, HEAD_DIM:]).astype(jnp.bfloat16)
    for h in range(4):
        mixed[dp, :, h * HEAD_DIM : (h + 1) * HEAD_DIM] = heads[h * TOK_DEV : (h + 1) * TOK_DEV]
    for j in range(1, 8):
        send(mixed.at[dp], mixed.at[dp], mixed_s, mixed_r.at[j], place.dp_peer(j))
    pending.append((mixed.at[pl.ds(0, 7)], mixed_s))

    for j in range(8):
        if j == 1:
            work(2)
        there = lax.rem(dp + 8 - j, 8)
        if j:
            arrive(mixed.at[there], mixed_r.at[j], place)
        out = nn(mixed[there], w_output[...])

        @pl.when(there == tp)
        def _():
            part_f[...] = out

        @pl.when(there != tp)
        def _():
            part_out[there] = out.astype(jnp.bfloat16)
            send(part_out.at[there], part_in.at[tp], part_s, part_r, (place.m, there, dp))

    pending.append((part_out.at[pl.ds(0, 7)], part_s))
    work(1)

    @pl.when(dp != tp)
    def _():
        arrive(raw, raw_r, place)

    total = part_f[...]
    arrive(part_in.at[pl.ds(0, 7)], part_r, place)
    for j in range(1, 8):
        total = total + part_in[lax.rem(tp + j, 8)].astype(jnp.float32)

    @pl.when(dp == tp)
    def _():
        for j in range(1, 8):
            pltpu.make_async_remote_copy(
                src_ref=res.at[:, columns(lax.rem(dp + j, 8))], dst_ref=raw, send_sem=raw_s.at[j], recv_sem=raw_r,
                device_id=place.dp_peer(j), device_id_type=pl.DeviceIdType.MESH,
            ).wait_send()

    pair.wait_send()
    for ref, sem in pending:
        arrive(ref, sem, place)
    return (raw[...].astype(jnp.float32) + total).astype(jnp.bfloat16)


def column_of(row):
    return jnp.broadcast_to(row, (128, 128)).T[:, :1]


def row_of(column):
    return jnp.broadcast_to(column, (128, 128)).T[:1]


SPLIT = 64
ORDER = "a1 n a1 n a1 b1 n b1 n a1 b1 a6 b5 a1 b2 a2 b1 a1 b1 a1 b2 a1 b1 a2 b3"


def step_kernel(
    res, gain, w_query, w_key, w_value, w_output, lengths, freq, w_hbm, enc_ref, dec_ref,
    rows_hbm, errs_hbm, w_out, act_t, pre_t, scale_ref, genc_ref,
    nsend, moved, raw, pair_out, pair_in, own_sum, qkv_out, qkv_in, kv, mixed, part_f, part_out, part_in,
    own_ref, rows, errs, w_raw, w, sums, give, taken, landing, result, total, act, slope, norms, latsum, gsum,
    moved_s, moved_r, raw_s, raw_r, pair_s, pair_r, qkv_s, qkv_r, kv_s, kv_r, mixed_s, mixed_r, part_s, part_r,
    w_sem, rows_send, rows_recv, rows_give, rows_take, errs_send, errs_recv, errs_give, errs_take,
    sum_send, sum_recv, pair_send, pair_recv, out_sem,
):
    place = Place()
    m, core = place.m, place.core
    loads = [
        pltpu.make_async_copy(w_hbm.at[pl.ds(i * SPLIT, SPLIT)], w_raw.at[i % 2], w_sem.at[i % 2])
        for i in range(BLOCK // SPLIT)
    ]
    loads[0].start()
    loads[1].start()
    done = [0]

    def work(count):
        for i in range(done[0], done[0] + count):
            at = pl.ds(i * SPLIT, SPLIT)
            loads[i].wait()

            def step(k, carry):
                cols = pl.ds(pl.multiple_of(k * BLOCK, BLOCK), BLOCK)
                for mm in (0, 1):
                    w[mm, at, cols] = w_raw[i % 2, :, mm, cols]
                return carry

            lax.fori_loop(0, 8, step, 0)
            if i + 2 < len(loads):
                loads[i + 2].start()
        done[0] += count

    layer_bufs = (nsend, moved, raw, pair_out, pair_in, own_sum, qkv_out, qkv_in, kv, mixed, part_f, part_out, part_in)
    layer_sems = (moved_s, moved_r, raw_s, raw_r, pair_s, pair_r, qkv_s, qkv_r, kv_s, kv_r, mixed_s, mixed_r, part_s, part_r)
    layer_refs = (res, gain, w_query, w_key, w_value, w_output, lengths, freq)
    own_ref[...] = attend_layer(place, layer_refs, layer_bufs, layer_sems, work)
    outs = [pltpu.make_async_copy(w, w_out, out_sem.at[4])]
    outs[0].start()
    own = (lax.div(place.at["z"], 2), m, place.at["y"], place.at["x"])
    for h in (0, 1):
        rows[(core, h) + own] = own_ref[h * HALF : (h + 1) * HALF, :]
    rows_sems = (rows_send, rows_recv, rows_give, rows_take)
    errs_sems = (errs_send, errs_recv, errs_give, errs_take)
    pending = []

    def norm_rows(first, count):
        def step(i, carry):
            at = pl.ds(pl.multiple_of(i * 16, 16), 16)
            for mm in (0, 1):
                wide = w[mm, at, :].astype(jnp.float32)
                norms[mm, at, :] = jnp.sqrt(jnp.sum(wide * wide, -1, keepdims=True) + 1e-06)
            return carry

        lax.fori_loop(first, first + count, step, 0)

    def contract(h, buf, first, count):
        if first == 0:
            total[h] = jnp.zeros((BLOCK, HALF_TOKENS), jnp.float32)

        def step(k, carry):
            mm, x, c, cols = chunk_of(k)
            total[h] += nt(w[mm, :, cols], token_rows(buf, h, mm, x, c))
            return carry

        lax.fori_loop(first, first + count, step, 0)

    def decode(h, mm, x, c):
        cols = pl.ds(pl.multiple_of((x * 2 + c) * BLOCK, BLOCK), BLOCK)
        return nn(act[h], w[mm, :, cols])

    blocked = (2, RING, HALF, BLOCK)

    def half_step(h):
        tokens = pl.ds(h * HALF_TOKENS, HALF_TOKENS)
        yield from gather(place, h, rows, rows_sems, pending)
        outs.append(pltpu.make_async_copy(rows.at[:, h], rows_hbm.at[:, h], out_sem.at[h]))
        outs[-1].start()
        contract(h, rows, 0, 8)
        yield
        contract(h, rows, 8, 8)
        for i in range(4):
            at = pl.ds(i * 128, 128)
            lat, slope[h, at, :] = gelu_pair(total[h, at, :] + column_of(enc_ref[i : i + 1, :]))
            latsum[h, at, :] = jnp.sum(lat, -1, keepdims=True)
            act_t[at, tokens] = lat.astype(jnp.bfloat16)
            act[h, :, at] = lat.T.astype(jnp.bfloat16)
        yield
        pairs = []
        for k in range(8):
            mm, x = k // 4, k % 4
            give[h, :, mm, :, x] = decode(h, mm, x, 1 - core).astype(jnp.bfloat16).reshape(blocked)
            ref = (h, slice(None), mm, slice(None), x)
            pairs.append(send(give.at[ref], taken.at[ref], pair_send.at[h, k], pair_recv.at[h, k], place.sibling()))
            if k % 4 == 3:
                yield
        for k in range(8):
            mm, x = k // 4, k % 4
            here = decode(h, mm, x, core)
            pairs[k].wait_recv()
            there = taken[h, :, mm, :, x].reshape(HALF_TOKENS, BLOCK).astype(jnp.float32)
            sums[h, :, mm, :, x] = (here + there).astype(jnp.bfloat16).reshape(blocked)
            if k == 3:
                yield
        pending.extend((give.at[h, :, 0, :, 0], pair_send.at[h, k]) for k in range(8))
        yield from scatter_sum(place, h, sums, landing, result, (sum_send, sum_recv), pending)
        bias = dec_ref[pl.ds(m * 8 + place.dp, 1), :]
        target = own_ref[h * HALF : (h + 1) * HALF, :].astype(jnp.float32)
        errs[(core, h) + own] = (result[h] + bias - target).astype(jnp.bfloat16)
        yield from gather(place, h, errs, errs_sems, pending)
        outs.append(pltpu.make_async_copy(errs.at[:, h], errs_hbm.at[:, h], out_sem.at[2 + h]))
        outs[-1].start()
        contract(h, errs, 0, 8)
        yield
        contract(h, errs, 8, 8)
        for i in range(4):
            at = pl.ds(i * 128, 128)
            norm_total = norms[0, at, :] + norms[1, at, :]
            pre_grad = (2.0 / TOKENS * total[h, at, :] + sparsity / TOKENS * norm_total) * slope[h, at, :]
            gsum[h, at, :] = jnp.sum(pre_grad, -1, keepdims=True)
            pre_t[at, tokens] = pre_grad.astype(jnp.bfloat16)

    halves = {"a": half_step(0), "b": half_step(1)}
    normed = 0
    for turn in ORDER.split():
        if turn == "n":
            norm_rows(8 * normed, 8)
            normed += 1
        else:
            for _ in range(int(turn[1:])):
                next(halves[turn[0]], None)
    for i in range(4):
        at = pl.ds(i * 128, 128)
        genc_ref[i : i + 1, :] = row_of(gsum[0, at, :] + gsum[1, at, :])
    scale_ref[...] = sparsity / TOKENS * (latsum[0] + latsum[1]) / norms[...]
    for copy in outs:
        copy.wait()
    for ref, sem in pending:
        arrive(ref, sem, place)


def grad_kernel(rows, errs, w, act_t, pre_t, scale, genc, gw, genc_out, gdec):
    for mm in (0, 1):
        err = errs[0, :, :, mm, :, 0].reshape(TOKENS, BLOCK)
        grad = 2.0 / TOKENS * nn(act_t[...], err) + nn(pre_t[...], rows[0, :, :, mm, :, 0].reshape(TOKENS, BLOCK))
        gw[:, mm, :] = (grad + scale[mm] * w[mm].astype(jnp.float32)).astype(jnp.bfloat16)
        ones = jnp.ones((16, TOKENS), jnp.bfloat16)
        gdec[mm : mm + 1, :] = 2.0 / TOKENS * nn(ones, err)[:1]
    genc_out[...] = genc[...]


def shards(
    residual, norm_gain, w_query, w_key, w_value, w_output, doc_lengths, coder_weight, enc_bias, dec_bias
):
    latents, _, features = coder_weight.shape
    blocks = (2, 2, 2, RING, RING, HALF, BLOCK)
    bf16, f32 = jnp.bfloat16, jnp.float32
    dma, vm = pltpu.SemaphoreType.DMA, pltpu.VMEM
    vmem = pl.BlockSpec(memory_space=pltpu.VMEM)
    hbm = pl.BlockSpec(memory_space=pl.ANY)
    ring = [dma((2, 3)), dma((2, 3, RING)), dma((2,)), dma((2,))]
    half = np.arange(HEAD_DIM // 2)
    freq = np.concatenate([rope_base ** (-half * 2.0 / HEAD_DIM)] * 2)[None].astype(np.float32)
    block = (TOK_DEV, BLOCK)
    rows, errs, w_t, act_t, pre_t, scale, genc = pl.pallas_call(
        step_kernel,
        out_shape=(
            jax.ShapeDtypeStruct((2,) + blocks, bf16),
            jax.ShapeDtypeStruct((2,) + blocks, bf16),
            jax.ShapeDtypeStruct((2, latents, features), bf16),
            jax.ShapeDtypeStruct((latents, TOKENS), bf16),
            jax.ShapeDtypeStruct((latents, TOKENS), bf16),
            jax.ShapeDtypeStruct((2, latents, 1), f32),
            jax.ShapeDtypeStruct((4, 128), f32),
        ),
        in_specs=[vmem] * 6 + [pl.BlockSpec(memory_space=pltpu.SMEM), vmem, hbm, vmem, vmem],
        out_specs=(hbm, hbm, hbm, vmem, vmem, vmem, vmem),
        scratch_shapes=[
            vm((8,) + block, bf16),
            vm((2, RING) + block, bf16),
            vm(block, bf16),
            vm((RING, TOK_DEV, 768), f32),
            vm((RING, TOK_DEV, 768), f32),
            vm((RING, TOK_DEV, 768), f32),
            vm((RING, TOK_DEV, 768), bf16),
            vm((RING, TOK_DEV, 768), bf16),
            vm((8, TOK_DEV, 2 * HEAD_DIM), bf16),
            vm((8,) + block, bf16),
            vm(block, f32),
            vm((8,) + block, bf16),
            vm((8,) + block, bf16),
            vm(block, bf16),
            vm((2,) + blocks, bf16),
            vm((2,) + blocks, bf16),
            vm((2, SPLIT, 2, features), bf16),
            vm((2, latents, features), bf16),
            vm(blocks, bf16),
            vm(blocks, bf16),
            vm(blocks, bf16),
            vm(blocks, bf16),
            vm((2, HALF, BLOCK), f32),
            vm((2, latents, HALF_TOKENS), f32),
            vm((2, HALF_TOKENS, latents), bf16),
            vm((2, latents, HALF_TOKENS), f32),
            vm((2, latents, 1), f32),
            vm((2, latents, 1), f32),
            vm((2, latents, 1), f32),
            *[dma(()), dma(()), dma((8,)), dma(()), dma(()), dma(())],
            *[dma(()), dma(()), dma(()), dma(()), dma(()), dma((8,)), dma(()), dma(())],
            dma((2,)),
            *ring,
            *ring,
            dma((2, 3)),
            dma((2, 3)),
            dma((2, 8)),
            dma((2, 8)),
            dma((5,)),
        ],
        compiler_params=pltpu.CompilerParams(collective_id=0, has_side_effects=True, vmem_limit_bytes=62 * 1024 * 1024),
        cost_estimate=pl.CostEstimate(flops=6 * TOKENS * latents * 2 * features, bytes_accessed=40 << 20, transcendentals=0),
    )(
        residual[0], norm_gain, w_query[0], w_key[0], w_value[0], w_output[0], doc_lengths, jnp.asarray(freq),
        coder_weight, enc_bias.reshape(4, 128), dec_bias.reshape(16, BLOCK),
    )
    set_spec = pl.BlockSpec(
        (1, 2, 2, 2, RING, 1, HALF, BLOCK), lambda k: (lax.rem(k, 2), 0, 0, 0, 0, lax.div(k, 2), 0, 0)
    )
    whole = lambda *shape: pl.BlockSpec(shape, lambda k: (0,) * len(shape))
    weight_grad, grad_enc, grad_dec = pl.pallas_call(
        grad_kernel,
        grid=(8,),
        out_shape=(
            jax.ShapeDtypeStruct((latents, 2, features), bf16),
            jax.ShapeDtypeStruct((4, 128), f32),
            jax.ShapeDtypeStruct((2, features), f32),
        ),
        in_specs=[
            set_spec,
            set_spec,
            pl.BlockSpec((2, latents, BLOCK), lambda k: (0, 0, k)),
            whole(latents, TOKENS),
            whole(latents, TOKENS),
            whole(2, latents, 1),
            whole(4, 128),
        ],
        out_specs=(
            pl.BlockSpec((latents, 2, BLOCK), lambda k: (0, 0, k)),
            whole(4, 128),
            pl.BlockSpec((2, BLOCK), lambda k: (0, k)),
        ),
        compiler_params=pltpu.CompilerParams(vmem_limit_bytes=62 * 1024 * 1024),
    )(rows, errs, w_t, act_t, pre_t, scale, genc)
    return (weight_grad, grad_enc.reshape(-1), grad_dec)


def solution(mesh):
    return jax.shard_map(
        shards,
        mesh=mesh,
        in_specs=(
            P("grp", "dp", None),
            P("grp", None),
            P("grp", "dp", "tp"),
            P("grp", "dp", "tp"),
            P("grp", "dp", "tp"),
            P("grp", "tp", "dp"),
            P(),
            P(("grp", "tp", "dp"), None, None),
            P(("grp", "tp", "dp")),
            P(),
        ),
        out_specs=(P(("grp", "tp", "dp"), None, None), P(("grp", "tp", "dp")), P()),
        check_vma=False,
    )
```

```python
import functools
import jax
import jax.numpy as jnp
import numpy as np
from jax import lax
from jax.experimental import pallas as pl
from jax.experimental.pallas import tpu as pltpu
from jax.sharding import PartitionSpec as P

HEAD_DIM = 128
TOK_DEV = 64
TOKENS = 512
BLOCK = 512
RING = 4
HALF = TOK_DEV // 2
HALF_TOKENS = TOKENS // 2

sparsity = 1.0
rope_base = 500000.0

ROUTES = (((0, 16), (0, 384), "xyz"), ((16, 16), (0, 384), "yzx"), ((0, 32), (384, 128), "zxy"))


class Place:
    def __init__(self):
        self.m = lax.axis_index("grp")
        tp, dp = lax.axis_index("tp"), lax.axis_index("dp")
        self.tp, self.dp = tp, dp
        self.core = lax.rem(dp, 2)
        self.at = {"x": lax.div(dp, 2), "y": lax.div(tp, 2), "z": lax.rem(tp, 2) * 2 + self.m}

    def device(self, at, core):
        z = at["z"]
        return (lax.rem(z, 2), at["y"] * 2 + lax.div(z, 2), at["x"] * 2 + core)

    def beside(self, axis, step):
        return lax.rem(self.at[axis] + (step + RING), RING)

    def neighbour(self, axis, step):
        return self.device({**self.at, axis: self.beside(axis, step)}, self.core)

    def sibling(self):
        return self.device(self.at, 1 - self.core)

    def dp_peer(self, j):
        return (self.m, self.tp, lax.rem(self.dp + j, 8))

    def tp_peer(self, j):
        return (self.m, lax.rem(self.tp + j, 8), self.dp)

    def enter(self):
        barrier = pltpu.get_barrier_semaphore()
        peers = [self.dp_peer(j) for j in range(1, 8)] + [self.tp_peer(j) for j in range(1, 8)]
        for peer in peers + [self.neighbour("z", 1), self.neighbour("z", -1)]:
            pl.semaphore_signal(barrier, inc=1, device_id=peer, device_id_type=pl.DeviceIdType.MESH)
        pl.semaphore_wait(barrier, 16)


def part(buf, lead, sel, rows, cols):
    z = sel.get("z")
    if z is None:
        index = [slice(None), slice(None)]
    elif isinstance(z, int):
        index = [z // 2, z % 2]
    else:
        index = [lax.div(z, 2), lax.rem(z, 2)]
    index += [sel.get(axis, slice(None)) for axis in "yx"]
    return buf.at[tuple(lead) + tuple(index) + (pl.ds(*rows), pl.ds(*cols))]


def send(src, dst, send_sem, recv_sem, device):
    copy = pltpu.make_async_remote_copy(
        src_ref=src, dst_ref=dst, send_sem=send_sem, recv_sem=recv_sem, device_id=device, device_id_type=pl.DeviceIdType.MESH
    )
    copy.start()
    return copy


def arrive(dst, sem, place):
    pltpu.make_async_remote_copy(
        src_ref=dst, dst_ref=dst, send_sem=sem, recv_sem=sem, device_id=place.sibling(), device_id_type=pl.DeviceIdType.MESH
    ).wait_recv()


def gather(place, h, buf, sems, pending):
    send_sems, recv_sems, give_sems, take_sems = sems
    mine = (place.core, h)

    def sel_of(order, k, v):
        return {order[k]: v, **{axis: place.at[axis] for axis in order[k + 1 :]}}

    def give(j):
        for rows, cols, order in ROUTES:
            ref = part(buf, mine, sel_of(order, 2, place.beside(order[2], -j)), rows, cols)
            send(ref, ref, give_sems.at[h], take_sems.at[h], place.sibling())

    one_ring = [buf.at[mine + (0,) * (4 - k)] for k in (0, 1, 2)]
    three_rings = [buf.at[mine + (0, 0, 0, pl.ds(0, 3))], buf.at[mine + (0, 0, pl.ds(0, 3))], buf.at[mine + (slice(None), slice(None), pl.ds(0, 3))]]
    for k in range(3):
        for j in (2, 1, 3):
            for rows, cols, order in ROUTES:
                ref = part(buf, mine, sel_of(order, k, place.at[order[k]]), rows, cols)
                send(ref, ref, send_sems.at[h, k], recv_sems.at[h, k, j], place.neighbour(order[k], j))
        pending.append((three_rings[k], send_sems.at[h, k]))
        if k == 2:
            give(0)
        yield
        for j in (1, 3, 2):
            arrive(one_ring[k], recv_sems.at[h, k, j], place)
            if k == 2:
                give(j)
    pending.append((buf.at[mine], give_sems.at[h]))


def spread(sel, i):
    at, rest = {}, i
    for axis in "xyz":
        if sel.get(axis) is None:
            at[axis] = lax.rem(rest, RING)
            rest = lax.div(rest, RING)
        else:
            at[axis] = sel[axis]
    z = at["z"]
    zh, zl = (z // 2, z % 2) if isinstance(z, int) else (lax.div(z, 2), lax.rem(z, 2))
    return zh, zl, at["y"], at["x"]


def scatter_sum(place, h, sums, landing, result, sems, pending):
    send_sems, recv_sems = sems

    def sel_of(order, k, v, done):
        return {order[k]: v, **{axis: place.at[axis] if done is None else done for axis in order[:k]}}

    def add(order, k, rows, cols):
        window = (pl.ds(*rows), pl.ds(*cols))

        def step(i, carry):
            own = (h,) + spread(sel_of(order, k, place.at[order[k]], None), i) + window
            total = sums[own].astype(jnp.float32)
            for j in range(1, RING):
                total = total + landing[(h,) + spread(sel_of(order, k, j, 0), i) + window].astype(jnp.float32)
            if k == 2:
                result[(h,) + window] = total
            else:
                sums[own] = total.astype(jnp.bfloat16)
            return carry

        lax.fori_loop(0, RING ** (2 - k), step, 0)

    three_rings = [landing.at[h, :, :, pl.ds(0, 3)], landing.at[h, 0, 0, pl.ds(0, 3)], landing.at[h, 0, 0, 0, pl.ds(0, 3)]]
    for k in range(3):
        for j in (2, 1, 3):
            for rows, cols, order in ROUTES:
                src = part(sums, (h,), sel_of(order, k, place.beside(order[k], j), None), rows, cols)
                dst = part(landing, (h,), sel_of(order, k, j, 0), rows, cols)
                send(src, dst, send_sems.at[h, k], recv_sems.at[h, k], place.neighbour(order[k], j))
        pending.append((three_rings[k], send_sems.at[h, k]))
        yield
        arrive(three_rings[k], recv_sems.at[h, k], place)
        for rows, cols, order in ROUTES:
            add(order, k, rows, cols)


def gelu_pair(pre_act):
    normal_cdf = 0.5 * (1.0 + lax.erf(pre_act * 0.7071067811865476))
    density = jnp.exp(-0.5 * pre_act * pre_act) * 0.3989422804014327
    return (pre_act * normal_cdf, normal_cdf + pre_act * density)


def nt(a, b):
    return lax.dot_general(a, b, (((1,), (1,)), ((), ())), preferred_element_type=jnp.float32)


def nn(a, b):
    return lax.dot_general(a, b, (((1,), (0,)), ((), ())), preferred_element_type=jnp.float32)


def token_rows(buf, h, mm, x, c):
    return buf[c, h, :, mm, :, x].reshape(HALF_TOKENS, BLOCK)


def doc_layout(lengths, token_index):
    doc, start, end = jnp.zeros_like(token_index), jnp.zeros_like(token_index), 0
    for i in range(4):
        end = end + lengths[i]
        passed = (token_index >= end).astype(jnp.int32)
        doc, start = doc + passed, start + passed * lengths[i]
    return doc, token_index - start


def attend_layer(place, refs, bufs, sems, work):
    res, gain, w_query, w_key, w_value, w_output, lengths, freq = refs
    nsend, moved, raw, pair_out, pair_in, own_sum, qkv_out, qkv_in, kv, mixed, part_f, part_out, part_in = bufs
    moved_s, moved_r, raw_s, raw_r, pair_s, pair_r, qkv_s, qkv_r, kv_s, kv_r, mixed_s, mixed_r, part_s, part_r = sems
    dp, tp, core, x = place.dp, place.tp, place.core, place.at["x"]
    pending = []

    for r in range(0, TOK_DEV, 16):
        wide = res[r : r + 16, :].astype(jnp.float32)
        scale = lax.rsqrt(jnp.mean(wide * wide, -1, keepdims=True) + 1e-05)
        normed = (wide * scale * gain[...].astype(jnp.float32)).astype(jnp.bfloat16)
        for d in range(8):
            nsend[d, r : r + 16, :] = normed[:, d * BLOCK : (d + 1) * BLOCK]
    place.enter()
    for j in range(1, 8):
        there = lax.rem(dp + j, 8)
        send(nsend.at[there], moved.at[core, x], moved_s, moved_r, place.dp_peer(j))
    pending.append((nsend.at[pl.ds(0, 7)], moved_s))
    moved[core, x] = nsend[dp]

    def columns(d):
        return pl.ds(pl.multiple_of(d * BLOCK, BLOCK), BLOCK)

    @pl.when(dp == tp)
    def _():
        for j in range(1, 8):
            send(res.at[:, columns(lax.rem(dp + j, 8))], raw, raw_s.at[j], raw_r, place.dp_peer(j))
        raw[...] = res[:, columns(dp)]

    here = dp * TOK_DEV + lax.broadcasted_iota(jnp.int32, (TOK_DEV, 1), 0)
    keys_at = lax.broadcasted_iota(jnp.int32, (1, TOKENS), 1)
    doc, pos = doc_layout(lengths, here)
    key_doc, _ = doc_layout(lengths, keys_at)
    angles = pos.astype(jnp.float32) * freq[...]
    lane = lax.broadcasted_iota(jnp.int32, (1, HEAD_DIM), 1)
    cosine = jnp.cos(angles)
    sine = jnp.sin(angles) * jnp.where(lane < HEAD_DIM // 2, -1.0, 1.0)
    allowed = (doc == key_doc) & (keys_at <= here)
    work(2)

    arrive(nsend.at[pl.ds(0, 7)], moved_r, place)

    def project(c, out):
        rows_in = moved[c].reshape(RING * TOK_DEV, BLOCK)
        for w_ref, at, width in ((w_query, 0, 512), (w_key, 512, 128), (w_value, 640, 128)):
            out[:, :, at : at + width] = nn(rows_in, w_ref[...]).reshape(RING, TOK_DEV, width)

    project(1 - core, pair_out)
    pair = send(pair_out, pair_in, pair_s, pair_r, place.sibling())
    project(core, own_sum)
    pair.wait_recv()
    own_sum[...] = own_sum[...] + pair_in[...]
    qkv_out[...] = own_sum[...].astype(jnp.bfloat16)
    for j in range(1, RING):
        there = lax.rem(x + j, RING)
        send(qkv_out.at[there], qkv_in.at[j], qkv_s, qkv_r, place.dp_peer(2 * j))
    pending.append((qkv_out.at[pl.ds(1, 3)], qkv_s))
    work(2)
    summed = own_sum[x]
    arrive(qkv_in.at[pl.ds(1, 3)], qkv_r, place)
    for j in range(1, RING):
        summed = summed + qkv_in[j].astype(jnp.float32)

    def rotate(values):
        return (values * cosine + pltpu.roll(values, HEAD_DIM // 2, 1) * sine).astype(jnp.bfloat16)

    kv[dp, :, :HEAD_DIM] = rotate(summed[:, 512:640])
    kv[dp, :, HEAD_DIM:] = summed[:, 640:].astype(jnp.bfloat16)
    for j in range(1, 8):
        send(kv.at[dp], kv.at[dp], kv_s, kv_r, place.dp_peer(j))
    pending.append((kv.at[pl.ds(0, 7)], kv_s))
    query = jnp.concatenate([rotate(summed[:, h * HEAD_DIM : (h + 1) * HEAD_DIM]) for h in range(4)], 0)
    work(1)
    arrive(kv.at[pl.ds(0, 7)], kv_r, place)

    all_kv = kv[...].reshape(TOKENS, 2 * HEAD_DIM)
    scores = nt(query, all_kv[:, :HEAD_DIM]) * HEAD_DIM ** (-0.5)
    mask = jnp.concatenate([allowed] * 4, 0)
    terms = jnp.where(mask, jnp.exp(jnp.where(mask, scores, 0.0)), 0.0)
    weights = (terms / jnp.sum(terms, -1, keepdims=True)).astype(jnp.bfloat16)
    heads = nn(weights, all_kv[:, HEAD_DIM:]).astype(jnp.bfloat16)
    for h in range(4):
        mixed[dp, :, h * HEAD_DIM : (h + 1) * HEAD_DIM] = heads[h * TOK_DEV : (h + 1) * TOK_DEV]
    for j in range(1, 8):
        send(mixed.at[dp], mixed.at[dp], mixed_s, mixed_r.at[j], place.dp_peer(j))
    pending.append((mixed.at[pl.ds(0, 7)], mixed_s))

    for j in range(8):
        if j == 1:
            work(2)
        there = lax.rem(dp + 8 - j, 8)
        if j:
            arrive(mixed.at[there], mixed_r.at[j], place)
        out = nn(mixed[there], w_output[...])

        @pl.when(there == tp)
        def _():
            part_f[...] = out

        @pl.when(there != tp)
        def _():
            part_out[there] = out.astype(jnp.bfloat16)
            send(part_out.at[there], part_in.at[tp], part_s, part_r, (place.m, there, dp))

    pending.append((part_out.at[pl.ds(0, 7)], part_s))
    work(1)

    @pl.when(dp != tp)
    def _():
        arrive(raw, raw_r, place)

    total = part_f[...]
    arrive(part_in.at[pl.ds(0, 7)], part_r, place)
    for j in range(1, 8):
        total = total + part_in[lax.rem(tp + j, 8)].astype(jnp.float32)

    @pl.when(dp == tp)
    def _():
        for j in range(1, 8):
            pltpu.make_async_remote_copy(
                src_ref=res.at[:, columns(lax.rem(dp + j, 8))], dst_ref=raw, send_sem=raw_s.at[j], recv_sem=raw_r,
                device_id=place.dp_peer(j), device_id_type=pl.DeviceIdType.MESH,
            ).wait_send()

    pair.wait_send()
    for ref, sem in pending:
        arrive(ref, sem, place)
    return (raw[...].astype(jnp.float32) + total).astype(jnp.bfloat16)


def column_of(row):
    return jnp.broadcast_to(row, (128, 128)).T[:, :1]


def row_of(column):
    return jnp.broadcast_to(column, (128, 128)).T[:1]


SPLIT = 64
ORDER = "a1 n a1 b1 n a1 b1 b1 n a1 a5 b1 n b3 a1 b2 a2 b1 a1 b1 a1 b3 a2 b2"


def step_kernel(
    res, gain, w_query, w_key, w_value, w_output, lengths, freq, w_hbm, enc_ref, dec_ref,
    rows_hbm, errs_hbm, w_out, act_t, pre_t, scale_ref, genc_ref,
    nsend, moved, raw, pair_out, pair_in, own_sum, qkv_out, qkv_in, kv, mixed, part_f, part_out, part_in,
    own_ref, rows, errs, w_raw, w, sums, give, taken, landing, result, total, act, slope, norms, latsum, gsum,
    moved_s, moved_r, raw_s, raw_r, pair_s, pair_r, qkv_s, qkv_r, kv_s, kv_r, mixed_s, mixed_r, part_s, part_r,
    w_sem, rows_send, rows_recv, rows_give, rows_take, errs_send, errs_recv, errs_give, errs_take,
    sum_send, sum_recv, pair_send, pair_recv, out_sem,
):
    place = Place()
    m, core = place.m, place.core
    loads = [
        pltpu.make_async_copy(w_hbm.at[pl.ds(i * SPLIT, SPLIT)], w_raw.at[i % 2], w_sem.at[i % 2])
        for i in range(BLOCK // SPLIT)
    ]
    loads[0].start()
    loads[1].start()
    done = [0]

    def work(count):
        for i in range(done[0], done[0] + count):
            at = pl.ds(i * SPLIT, SPLIT)
            loads[i].wait()

            def step(k, carry):
                cols = pl.ds(pl.multiple_of(k * BLOCK, BLOCK), BLOCK)
                for mm in (0, 1):
                    w[mm, at, cols] = w_raw[i % 2, :, mm, cols]
                return carry

            lax.fori_loop(0, 8, step, 0)
            if i + 2 < len(loads):
                loads[i + 2].start()
        done[0] += count

    layer_bufs = (nsend, moved, raw, pair_out, pair_in, own_sum, qkv_out, qkv_in, kv, mixed, part_f, part_out, part_in)
    layer_sems = (moved_s, moved_r, raw_s, raw_r, pair_s, pair_r, qkv_s, qkv_r, kv_s, kv_r, mixed_s, mixed_r, part_s, part_r)
    layer_refs = (res, gain, w_query, w_key, w_value, w_output, lengths, freq)
    own_ref[...] = attend_layer(place, layer_refs, layer_bufs, layer_sems, work)
    outs = [pltpu.make_async_copy(w, w_out, out_sem.at[4])]
    outs[0].start()
    own = (lax.div(place.at["z"], 2), m, place.at["y"], place.at["x"])
    for h in (0, 1):
        rows[(core, h) + own] = own_ref[h * HALF : (h + 1) * HALF, :]
    rows_sems = (rows_send, rows_recv, rows_give, rows_take)
    errs_sems = (errs_send, errs_recv, errs_give, errs_take)
    pending = []

    def norm_rows(first, count):
        def step(i, carry):
            at = pl.ds(pl.multiple_of(i * 16, 16), 16)
            for mm in (0, 1):
                wide = w[mm, at, :].astype(jnp.float32)
                norms[mm, at, :] = jnp.sqrt(jnp.sum(wide * wide, -1, keepdims=True) + 1e-06)
            return carry

        lax.fori_loop(first, first + count, step, 0)

    def contract(h, buf, c, fresh):
        if fresh:
            total[h] = jnp.zeros((BLOCK, HALF_TOKENS), jnp.float32)

        def step(k, carry):
            mm, x = lax.div(k, RING), lax.rem(k, RING)
            cols = pl.ds(pl.multiple_of((x * 2 + c) * BLOCK, BLOCK), BLOCK)
            total[h] += nt(w[mm, :, cols], token_rows(buf, h, mm, x, c))
            return carry

        lax.fori_loop(0, 2 * RING, step, 0)

    def contract_all(h, buf, take_sems, first_out):
        contract(h, buf, core, True)
        yield
        arrive(buf.at[1 - core, h], take_sems.at[h], place)
        out_hbm = (rows_hbm, errs_hbm)[first_out // 2]
        outs.append(pltpu.make_async_copy(buf.at[:, h], out_hbm.at[:, h], out_sem.at[first_out + h]))
        outs[-1].start()
        contract(h, buf, 1 - core, False)

    def decode(h, mm, x, c):
        cols = pl.ds(pl.multiple_of((x * 2 + c) * BLOCK, BLOCK), BLOCK)
        return nn(act[h], w[mm, :, cols])

    blocked = (2, RING, HALF, BLOCK)

    def half_step(h):
        tokens = pl.ds(h * HALF_TOKENS, HALF_TOKENS)
        yield from gather(place, h, rows, rows_sems, pending)
        yield from contract_all(h, rows, rows_take, 0)
        for i in range(4):
            at = pl.ds(i * 128, 128)
            lat, slope[h, at, :] = gelu_pair(total[h, at, :] + column_of(enc_ref[i : i + 1, :]))
            latsum[h, at, :] = jnp.sum(lat, -1, keepdims=True)
            act_t[at, tokens] = lat.astype(jnp.bfloat16)
            act[h, :, at] = lat.T.astype(jnp.bfloat16)
        yield
        pairs = []
        for k in range(8):
            mm, x = k // 4, k % 4
            give[h, :, mm, :, x] = decode(h, mm, x, 1 - core).astype(jnp.bfloat16).reshape(blocked)
            ref = (h, slice(None), mm, slice(None), x)
            pairs.append(send(give.at[ref], taken.at[ref], pair_send.at[h, k], pair_recv.at[h, k], place.sibling()))
            if k % 4 == 3:
                yield
        for k in range(8):
            mm, x = k // 4, k % 4
            here = decode(h, mm, x, core)
            pairs[k].wait_recv()
            there = taken[h, :, mm, :, x].reshape(HALF_TOKENS, BLOCK).astype(jnp.float32)
            sums[h, :, mm, :, x] = (here + there).astype(jnp.bfloat16).reshape(blocked)
            if k == 3:
                yield
        pending.extend((give.at[h, :, 0, :, 0], pair_send.at[h, k]) for k in range(8))
        yield from scatter_sum(place, h, sums, landing, result, (sum_send, sum_recv), pending)
        bias = dec_ref[pl.ds(m, 1), pl.ds(pl.multiple_of(place.dp * BLOCK, BLOCK), BLOCK)]
        target = own_ref[h * HALF : (h + 1) * HALF, :].astype(jnp.float32)
        errs[(core, h) + own] = (result[h] + bias - target).astype(jnp.bfloat16)
        yield from gather(place, h, errs, errs_sems, pending)
        yield from contract_all(h, errs, errs_take, 2)
        for i in range(4):
            at = pl.ds(i * 128, 128)
            norm_total = norms[0, at, :] + norms[1, at, :]
            pre_grad = (2.0 / TOKENS * total[h, at, :] + sparsity / TOKENS * norm_total) * slope[h, at, :]
            gsum[h, at, :] = jnp.sum(pre_grad, -1, keepdims=True)
            pre_t[at, tokens] = pre_grad.astype(jnp.bfloat16)

    halves = {"a": half_step(0), "b": half_step(1)}
    normed = 0
    for turn in ORDER.split():
        if turn == "n":
            norm_rows(8 * normed, 8)
            normed += 1
        else:
            for _ in range(int(turn[1:])):
                next(halves[turn[0]], None)
    for i in range(4):
        at = pl.ds(i * 128, 128)
        genc_ref[i : i + 1, :] = row_of(gsum[0, at, :] + gsum[1, at, :])
    scale_ref[...] = sparsity / TOKENS * (latsum[0] + latsum[1]) / norms[...]
    for copy in outs:
        copy.wait()
    for ref, sem in pending:
        arrive(ref, sem, place)


def grad_kernel(rows, errs, w, act_t, pre_t, scale, genc, gw, genc_out, gdec):
    for mm in (0, 1):
        err = errs[0, :, :, mm, :, 0].reshape(TOKENS, BLOCK)
        grad = 2.0 / TOKENS * nn(act_t[...], err) + nn(pre_t[...], rows[0, :, :, mm, :, 0].reshape(TOKENS, BLOCK))
        gw[:, mm, :] = (grad + scale[mm] * w[mm].astype(jnp.float32)).astype(jnp.bfloat16)
        ones = jnp.ones((16, TOKENS), jnp.bfloat16)
        gdec[mm : mm + 1, :] = 2.0 / TOKENS * nn(ones, err)[:1]
    genc_out[...] = genc[...]


def shards(
    residual, norm_gain, w_query, w_key, w_value, w_output, doc_lengths, coder_weight, enc_bias, dec_bias
):
    latents, _, features = coder_weight.shape
    blocks = (2, 2, 2, RING, RING, HALF, BLOCK)
    bf16, f32 = jnp.bfloat16, jnp.float32
    dma, vm = pltpu.SemaphoreType.DMA, pltpu.VMEM
    vmem = pl.BlockSpec(memory_space=pltpu.VMEM)
    hbm = pl.BlockSpec(memory_space=pl.ANY)
    ring = [dma((2, 3)), dma((2, 3, RING)), dma((2,)), dma((2,))]
    half = np.arange(HEAD_DIM // 2)
    freq = np.concatenate([rope_base ** (-half * 2.0 / HEAD_DIM)] * 2)[None].astype(np.float32)
    block = (TOK_DEV, BLOCK)
    rows, errs, w_t, act_t, pre_t, scale, genc = pl.pallas_call(
        step_kernel,
        out_shape=(
            jax.ShapeDtypeStruct((2,) + blocks, bf16),
            jax.ShapeDtypeStruct((2,) + blocks, bf16),
            jax.ShapeDtypeStruct((2, latents, features), bf16),
            jax.ShapeDtypeStruct((latents, TOKENS), bf16),
            jax.ShapeDtypeStruct((latents, TOKENS), bf16),
            jax.ShapeDtypeStruct((2, latents, 1), f32),
            jax.ShapeDtypeStruct((4, 128), f32),
        ),
        in_specs=[vmem] * 6 + [pl.BlockSpec(memory_space=pltpu.SMEM), vmem, hbm, vmem, vmem],
        out_specs=(hbm, hbm, hbm, vmem, vmem, vmem, vmem),
        scratch_shapes=[
            vm((8,) + block, bf16),
            vm((2, RING) + block, bf16),
            vm(block, bf16),
            vm((RING, TOK_DEV, 768), f32),
            vm((RING, TOK_DEV, 768), f32),
            vm((RING, TOK_DEV, 768), f32),
            vm((RING, TOK_DEV, 768), bf16),
            vm((RING, TOK_DEV, 768), bf16),
            vm((8, TOK_DEV, 2 * HEAD_DIM), bf16),
            vm((8,) + block, bf16),
            vm(block, f32),
            vm((8,) + block, bf16),
            vm((8,) + block, bf16),
            vm(block, bf16),
            vm((2,) + blocks, bf16),
            vm((2,) + blocks, bf16),
            vm((2, SPLIT, 2, features), bf16),
            vm((2, latents, features), bf16),
            vm(blocks, bf16),
            vm(blocks, bf16),
            vm(blocks, bf16),
            vm(blocks, bf16),
            vm((2, HALF, BLOCK), f32),
            vm((2, latents, HALF_TOKENS), f32),
            vm((2, HALF_TOKENS, latents), bf16),
            vm((2, latents, HALF_TOKENS), f32),
            vm((2, latents, 1), f32),
            vm((2, latents, 1), f32),
            vm((2, latents, 1), f32),
            *[dma(()), dma(()), dma((8,)), dma(()), dma(()), dma(())],
            *[dma(()), dma(()), dma(()), dma(()), dma(()), dma((8,)), dma(()), dma(())],
            dma((2,)),
            *ring,
            *ring,
            dma((2, 3)),
            dma((2, 3)),
            dma((2, 8)),
            dma((2, 8)),
            dma((5,)),
        ],
        compiler_params=pltpu.CompilerParams(collective_id=0, has_side_effects=True, vmem_limit_bytes=62 * 1024 * 1024),
        cost_estimate=pl.CostEstimate(flops=6 * TOKENS * latents * 2 * features, bytes_accessed=40 << 20, transcendentals=0),
    )(
        residual[0], norm_gain, w_query[0], w_key[0], w_value[0], w_output[0], doc_lengths, jnp.asarray(freq),
        coder_weight, enc_bias.reshape(4, 128), dec_bias,
    )
    set_spec = pl.BlockSpec(
        (1, 2, 2, 2, RING, 1, HALF, BLOCK), lambda k: (lax.rem(k, 2), 0, 0, 0, 0, lax.div(k, 2), 0, 0)
    )
    whole = lambda *shape: pl.BlockSpec(shape, lambda k: (0,) * len(shape))
    weight_grad, grad_enc, grad_dec = pl.pallas_call(
        grad_kernel,
        grid=(8,),
        out_shape=(
            jax.ShapeDtypeStruct((latents, 2, features), bf16),
            jax.ShapeDtypeStruct((4, 128), f32),
            jax.ShapeDtypeStruct((2, features), f32),
        ),
        in_specs=[
            set_spec,
            set_spec,
            pl.BlockSpec((2, latents, BLOCK), lambda k: (0, 0, k)),
            whole(latents, TOKENS),
            whole(latents, TOKENS),
            whole(2, latents, 1),
            whole(4, 128),
        ],
        out_specs=(
            pl.BlockSpec((latents, 2, BLOCK), lambda k: (0, 0, k)),
            whole(4, 128),
            pl.BlockSpec((2, BLOCK), lambda k: (0, k)),
        ),
        compiler_params=pltpu.CompilerParams(vmem_limit_bytes=62 * 1024 * 1024),
    )(rows, errs, w_t, act_t, pre_t, scale, genc)
    return (weight_grad, grad_enc.reshape(-1), grad_dec)


def solution(mesh):
    return jax.shard_map(
        shards,
        mesh=mesh,
        in_specs=(
            P("grp", "dp", None),
            P("grp", None),
            P("grp", "dp", "tp"),
            P("grp", "dp", "tp"),
            P("grp", "dp", "tp"),
            P("grp", "tp", "dp"),
            P(),
            P(("grp", "tp", "dp"), None, None),
            P(("grp", "tp", "dp")),
            P(),
        ),
        out_specs=(P(("grp", "tp", "dp"), None, None), P(("grp", "tp", "dp")), P()),
        check_vma=False,
    )
```

```python
import functools
import jax
import jax.numpy as jnp
import numpy as np
from jax import lax
from jax.experimental import pallas as pl
from jax.experimental.pallas import tpu as pltpu
from jax.sharding import PartitionSpec as P

HEAD_DIM = 128
TOK_DEV = 64
TOKENS = 512
BLOCK = 512
RING = 4
HALF = TOK_DEV // 2
HALF_TOKENS = TOKENS // 2

sparsity = 1.0
rope_base = 500000.0

ROUTES = (((0, 16), (0, 384), "xyz"), ((16, 16), (0, 384), "yzx"), ((0, 32), (384, 128), "zxy"))


class Place:
    def __init__(self):
        self.m = lax.axis_index("grp")
        tp, dp = lax.axis_index("tp"), lax.axis_index("dp")
        self.tp, self.dp = tp, dp
        self.core = lax.rem(dp, 2)
        self.at = {"x": lax.div(dp, 2), "y": lax.div(tp, 2), "z": lax.rem(tp, 2) * 2 + self.m}

    def device(self, at, core):
        z = at["z"]
        return (lax.rem(z, 2), at["y"] * 2 + lax.div(z, 2), at["x"] * 2 + core)

    def beside(self, axis, step):
        return lax.rem(self.at[axis] + (step + RING), RING)

    def neighbour(self, axis, step):
        return self.device({**self.at, axis: self.beside(axis, step)}, self.core)

    def sibling(self):
        return self.device(self.at, 1 - self.core)

    def dp_peer(self, j):
        return (self.m, self.tp, lax.rem(self.dp + j, 8))

    def tp_peer(self, j):
        return (self.m, lax.rem(self.tp + j, 8), self.dp)

    def enter(self):
        barrier = pltpu.get_barrier_semaphore()
        peers = [self.dp_peer(j) for j in range(1, 8)] + [self.tp_peer(j) for j in range(1, 8)]
        for peer in peers + [self.neighbour("z", 1), self.neighbour("z", -1)]:
            pl.semaphore_signal(barrier, inc=1, device_id=peer, device_id_type=pl.DeviceIdType.MESH)
        pl.semaphore_wait(barrier, 16)


def part(buf, lead, sel, rows, cols):
    z = sel.get("z")
    if z is None:
        index = [slice(None), slice(None)]
    elif isinstance(z, int):
        index = [z // 2, z % 2]
    else:
        index = [lax.div(z, 2), lax.rem(z, 2)]
    index += [sel.get(axis, slice(None)) for axis in "yx"]
    return buf.at[tuple(lead) + tuple(index) + (pl.ds(*rows), pl.ds(*cols))]


def send(src, dst, send_sem, recv_sem, device):
    copy = pltpu.make_async_remote_copy(
        src_ref=src, dst_ref=dst, send_sem=send_sem, recv_sem=recv_sem, device_id=device, device_id_type=pl.DeviceIdType.MESH
    )
    copy.start()
    return copy


def arrive(dst, sem, place):
    pltpu.make_async_remote_copy(
        src_ref=dst, dst_ref=dst, send_sem=sem, recv_sem=sem, device_id=place.sibling(), device_id_type=pl.DeviceIdType.MESH
    ).wait_recv()


def gather(place, h, buf, sems, pending):
    send_sems, recv_sems, give_sems, take_sems = sems
    mine = (place.core, h)

    def sel_of(order, k, v):
        return {order[k]: v, **{axis: place.at[axis] for axis in order[k + 1 :]}}

    def give(j):
        for rows, cols, order in ROUTES:
            ref = part(buf, mine, sel_of(order, 2, place.beside(order[2], -j)), rows, cols)
            send(ref, ref, give_sems.at[h], take_sems.at[h], place.sibling())

    one_ring = [buf.at[mine + (0,) * (4 - k)] for k in (0, 1, 2)]
    three_rings = [buf.at[mine + (0, 0, 0, pl.ds(0, 3))], buf.at[mine + (0, 0, pl.ds(0, 3))], buf.at[mine + (slice(None), slice(None), pl.ds(0, 3))]]
    for k in range(3):
        for j in (2, 1, 3):
            for rows, cols, order in ROUTES:
                ref = part(buf, mine, sel_of(order, k, place.at[order[k]]), rows, cols)
                send(ref, ref, send_sems.at[h, k], recv_sems.at[h, k, j], place.neighbour(order[k], j))
        pending.append((three_rings[k], send_sems.at[h, k]))
        if k == 2:
            give(0)
        yield
        for j in (1, 3, 2):
            arrive(one_ring[k], recv_sems.at[h, k, j], place)
            if k == 2:
                give(j)
    pending.append((buf.at[mine], give_sems.at[h]))


def spread(sel, i):
    at, rest = {}, i
    for axis in "xyz":
        if sel.get(axis) is None:
            at[axis] = lax.rem(rest, RING)
            rest = lax.div(rest, RING)
        else:
            at[axis] = sel[axis]
    z = at["z"]
    zh, zl = (z // 2, z % 2) if isinstance(z, int) else (lax.div(z, 2), lax.rem(z, 2))
    return zh, zl, at["y"], at["x"]


def scatter_sum(place, h, sums, landing, result, sems, pending):
    send_sems, recv_sems = sems

    def sel_of(order, k, v, done):
        return {order[k]: v, **{axis: place.at[axis] if done is None else done for axis in order[:k]}}

    def add(order, k, rows, cols):
        window = (pl.ds(*rows), pl.ds(*cols))

        def step(i, carry):
            own = (h,) + spread(sel_of(order, k, place.at[order[k]], None), i) + window
            total = sums[own].astype(jnp.float32)
            for j in range(1, RING):
                total = total + landing[(h,) + spread(sel_of(order, k, j, 0), i) + window].astype(jnp.float32)
            if k == 2:
                result[(h,) + window] = total
            else:
                sums[own] = total.astype(jnp.bfloat16)
            return carry

        lax.fori_loop(0, RING ** (2 - k), step, 0)

    three_rings = [landing.at[h, :, :, pl.ds(0, 3)], landing.at[h, 0, 0, pl.ds(0, 3)], landing.at[h, 0, 0, 0, pl.ds(0, 3)]]
    for k in range(3):
        for j in (2, 1, 3):
            for rows, cols, order in ROUTES:
                src = part(sums, (h,), sel_of(order, k, place.beside(order[k], j), None), rows, cols)
                dst = part(landing, (h,), sel_of(order, k, j, 0), rows, cols)
                send(src, dst, send_sems.at[h, k], recv_sems.at[h, k], place.neighbour(order[k], j))
        pending.append((three_rings[k], send_sems.at[h, k]))
        yield
        arrive(three_rings[k], recv_sems.at[h, k], place)
        for rows, cols, order in ROUTES:
            add(order, k, rows, cols)


def gelu_pair(pre_act):
    normal_cdf = 0.5 * (1.0 + lax.erf(pre_act * 0.7071067811865476))
    density = jnp.exp(-0.5 * pre_act * pre_act) * 0.3989422804014327
    return (pre_act * normal_cdf, normal_cdf + pre_act * density)


def nt(a, b):
    return lax.dot_general(a, b, (((1,), (1,)), ((), ())), preferred_element_type=jnp.float32)


def nn(a, b):
    return lax.dot_general(a, b, (((1,), (0,)), ((), ())), preferred_element_type=jnp.float32)


def token_rows(buf, h, mm, x, c):
    return buf[c, h, :, mm, :, x].reshape(HALF_TOKENS, BLOCK)


def doc_layout(lengths, token_index):
    doc, start, end = jnp.zeros_like(token_index), jnp.zeros_like(token_index), 0
    for i in range(4):
        end = end + lengths[i]
        passed = (token_index >= end).astype(jnp.int32)
        doc, start = doc + passed, start + passed * lengths[i]
    return doc, token_index - start


def attend_layer(place, refs, bufs, sems, work):
    res, gain, w_query, w_key, w_value, w_output, lengths, freq = refs
    nsend, moved, raw, pair_out, pair_in, own_sum, qkv_out, qkv_in, kv, mixed, part_f, part_out, part_in = bufs
    moved_s, moved_r, raw_s, raw_r, pair_s, pair_r, qkv_s, qkv_r, kv_s, kv_r, mixed_s, mixed_r, part_s, part_r = sems
    dp, tp, core, x = place.dp, place.tp, place.core, place.at["x"]
    pending = []

    for r in range(0, TOK_DEV, 16):
        wide = res[r : r + 16, :].astype(jnp.float32)
        scale = lax.rsqrt(jnp.mean(wide * wide, -1, keepdims=True) + 1e-05)
        normed = (wide * scale * gain[...].astype(jnp.float32)).astype(jnp.bfloat16)
        for d in range(8):
            nsend[d, r : r + 16, :] = normed[:, d * BLOCK : (d + 1) * BLOCK]
    place.enter()
    for j in range(1, 8):
        there = lax.rem(dp + j, 8)
        send(nsend.at[there], moved.at[core, x], moved_s, moved_r, place.dp_peer(j))
    pending.append((nsend.at[pl.ds(0, 7)], moved_s))
    moved[core, x] = nsend[dp]

    def columns(d):
        return pl.ds(pl.multiple_of(d * BLOCK, BLOCK), BLOCK)

    here = dp * TOK_DEV + lax.broadcasted_iota(jnp.int32, (TOK_DEV, 1), 0)
    keys_at = lax.broadcasted_iota(jnp.int32, (1, TOKENS), 1)
    doc, pos = doc_layout(lengths, here)
    key_doc, _ = doc_layout(lengths, keys_at)
    angles = pos.astype(jnp.float32) * freq[...]
    lane = lax.broadcasted_iota(jnp.int32, (1, HEAD_DIM), 1)
    cosine = jnp.cos(angles)
    sine = jnp.sin(angles) * jnp.where(lane < HEAD_DIM // 2, -1.0, 1.0)
    allowed = (doc == key_doc) & (keys_at <= here)
    work(4)

    arrive(nsend.at[pl.ds(0, 7)], moved_r, place)

    def project(c, out):
        rows_in = moved[c].reshape(RING * TOK_DEV, BLOCK)
        for w_ref, at, width in ((w_query, 0, 512), (w_key, 512, 128), (w_value, 640, 128)):
            out[:, :, at : at + width] = nn(rows_in, w_ref[...]).reshape(RING, TOK_DEV, width)

    project(1 - core, pair_out)
    pair = send(pair_out, pair_in, pair_s, pair_r, place.sibling())
    project(core, own_sum)
    pair.wait_recv()
    own_sum[...] = own_sum[...] + pair_in[...]
    qkv_out[...] = own_sum[...].astype(jnp.bfloat16)
    for j in range(1, RING):
        there = lax.rem(x + j, RING)
        send(qkv_out.at[there], qkv_in.at[j], qkv_s, qkv_r, place.dp_peer(2 * j))
    pending.append((qkv_out.at[pl.ds(1, 3)], qkv_s))
    work(2)
    summed = own_sum[x]
    arrive(qkv_in.at[pl.ds(1, 3)], qkv_r, place)
    for j in range(1, RING):
        summed = summed + qkv_in[j].astype(jnp.float32)

    def rotate(values):
        return (values * cosine + pltpu.roll(values, HEAD_DIM // 2, 1) * sine).astype(jnp.bfloat16)

    kv[dp, :, :HEAD_DIM] = rotate(summed[:, 512:640])
    kv[dp, :, HEAD_DIM:] = summed[:, 640:].astype(jnp.bfloat16)
    for j in range(1, 8):
        send(kv.at[dp], kv.at[dp], kv_s, kv_r, place.dp_peer(j))
    pending.append((kv.at[pl.ds(0, 7)], kv_s))

    @pl.when(dp == tp)
    def _():
        for j in range(1, 8):
            send(res.at[:, columns(lax.rem(dp + j, 8))], raw, raw_s.at[j], raw_r, place.dp_peer(j))
        raw[...] = res[:, columns(dp)]

    query = jnp.concatenate([rotate(summed[:, h * HEAD_DIM : (h + 1) * HEAD_DIM]) for h in range(4)], 0)
    work(2)
    arrive(kv.at[pl.ds(0, 7)], kv_r, place)

    all_kv = kv[...].reshape(TOKENS, 2 * HEAD_DIM)
    scores = nt(query, all_kv[:, :HEAD_DIM]) * HEAD_DIM ** (-0.5)
    mask = jnp.concatenate([allowed] * 4, 0)
    terms = jnp.where(mask, jnp.exp(jnp.where(mask, scores, 0.0)), 0.0)
    weights = (terms / jnp.sum(terms, -1, keepdims=True)).astype(jnp.bfloat16)
    heads = nn(weights, all_kv[:, HEAD_DIM:]).astype(jnp.bfloat16)
    for h in range(4):
        mixed[dp, :, h * HEAD_DIM : (h + 1) * HEAD_DIM] = heads[h * TOK_DEV : (h + 1) * TOK_DEV]
    sibling = dp + 1 - 2 * core
    send(mixed.at[dp], mixed.at[dp], mixed_s, mixed_r.at[1], place.sibling())
    for j in (2, 4, 6):
        send(mixed.at[dp], mixed.at[dp], mixed_s, mixed_r.at[j], place.dp_peer(j))
    pending.append((mixed.at[pl.ds(0, 7)], mixed_s))

    for j in (0, 1, 2, 6, 4, 3, 7, 5):
        if j == 1:
            there = sibling
        elif j % 2:
            there = lax.rem(sibling + 8 - (j - 1), 8)
        else:
            there = lax.rem(dp + 8 - j, 8)
        if j:
            arrive(mixed.at[there], mixed_r.at[j], place)
        if j in (2, 4, 6):
            send(mixed.at[there], mixed.at[there], mixed_s, mixed_r.at[j + 1], place.sibling())
        out = nn(mixed[there], w_output[...])

        @pl.when(there == tp)
        def _():
            part_f[...] = out

        @pl.when(there != tp)
        def _():
            part_out[there] = out.astype(jnp.bfloat16)
            send(part_out.at[there], part_in.at[tp], part_s, part_r, (place.m, there, dp))

    pending.append((part_out.at[pl.ds(0, 7)], part_s))

    @pl.when(dp != tp)
    def _():
        arrive(raw, raw_r, place)

    total = part_f[...]
    arrive(part_in.at[pl.ds(0, 7)], part_r, place)
    for j in range(1, 8):
        total = total + part_in[lax.rem(tp + j, 8)].astype(jnp.float32)

    @pl.when(dp == tp)
    def _():
        for j in range(1, 8):
            pltpu.make_async_remote_copy(
                src_ref=res.at[:, columns(lax.rem(dp + j, 8))], dst_ref=raw, send_sem=raw_s.at[j], recv_sem=raw_r,
                device_id=place.dp_peer(j), device_id_type=pl.DeviceIdType.MESH,
            ).wait_send()

    pair.wait_send()
    for ref, sem in pending:
        arrive(ref, sem, place)
    return (raw[...].astype(jnp.float32) + total).astype(jnp.bfloat16)


def column_of(row):
    return jnp.broadcast_to(row, (128, 128)).T[:, :1]


def row_of(column):
    return jnp.broadcast_to(column, (128, 128)).T[:1]


SPLIT = 64
ORDER = "a1 n a1 b1 n a1 b1 b1 n a1 a5 b1 n b3 a1 b2 a2 b1 a1 b1 a1 b3 a2 b2"


def step_kernel(
    res, gain, w_query, w_key, w_value, w_output, lengths, freq, w_hbm, enc_ref, dec_ref,
    rows_hbm, errs_hbm, w_out, act_t, pre_t, scale_ref, genc_ref,
    nsend, moved, raw, pair_out, pair_in, own_sum, qkv_out, qkv_in, kv, mixed, part_f, part_out, part_in,
    own_ref, rows, errs, w_raw, w, sums, give, taken, landing, result, total, act, slope, norms, latsum, gsum,
    moved_s, moved_r, raw_s, raw_r, pair_s, pair_r, qkv_s, qkv_r, kv_s, kv_r, mixed_s, mixed_r, part_s, part_r,
    w_sem, rows_send, rows_recv, rows_give, rows_take, errs_send, errs_recv, errs_give, errs_take,
    sum_send, sum_recv, pair_send, pair_recv, out_sem,
):
    place = Place()
    m, core = place.m, place.core
    loads = [
        pltpu.make_async_copy(w_hbm.at[pl.ds(i * SPLIT, SPLIT)], w_raw.at[i % 2], w_sem.at[i % 2])
        for i in range(BLOCK // SPLIT)
    ]
    loads[0].start()
    loads[1].start()
    done = [0]

    def work(count):
        for i in range(done[0], done[0] + count):
            at = pl.ds(i * SPLIT, SPLIT)
            loads[i].wait()

            def step(k, carry):
                cols = pl.ds(pl.multiple_of(k * BLOCK, BLOCK), BLOCK)
                for mm in (0, 1):
                    w[mm, at, cols] = w_raw[i % 2, :, mm, cols]
                return carry

            lax.fori_loop(0, 8, step, 0)
            if i + 2 < len(loads):
                loads[i + 2].start()
        done[0] += count

    layer_bufs = (nsend, moved, raw, pair_out, pair_in, own_sum, qkv_out, qkv_in, kv, mixed, part_f, part_out, part_in)
    layer_sems = (moved_s, moved_r, raw_s, raw_r, pair_s, pair_r, qkv_s, qkv_r, kv_s, kv_r, mixed_s, mixed_r, part_s, part_r)
    layer_refs = (res, gain, w_query, w_key, w_value, w_output, lengths, freq)
    own_ref[...] = attend_layer(place, layer_refs, layer_bufs, layer_sems, work)
    outs = [pltpu.make_async_copy(w, w_out, out_sem.at[4])]
    outs[0].start()
    own = (lax.div(place.at["z"], 2), m, place.at["y"], place.at["x"])
    for h in (0, 1):
        rows[(core, h) + own] = own_ref[h * HALF : (h + 1) * HALF, :]
    rows_sems = (rows_send, rows_recv, rows_give, rows_take)
    errs_sems = (errs_send, errs_recv, errs_give, errs_take)
    pending = []

    def norm_rows(first, count):
        def step(i, carry):
            at = pl.ds(pl.multiple_of(i * 16, 16), 16)
            for mm in (0, 1):
                wide = w[mm, at, :].astype(jnp.float32)
                norms[mm, at, :] = jnp.sqrt(jnp.sum(wide * wide, -1, keepdims=True) + 1e-06)
            return carry

        lax.fori_loop(first, first + count, step, 0)

    def contract(h, buf, c, fresh):
        if fresh:
            total[h] = jnp.zeros((BLOCK, HALF_TOKENS), jnp.float32)

        def step(k, carry):
            mm, x = lax.div(k, RING), lax.rem(k, RING)
            cols = pl.ds(pl.multiple_of((x * 2 + c) * BLOCK, BLOCK), BLOCK)
            total[h] += nt(w[mm, :, cols], token_rows(buf, h, mm, x, c))
            return carry

        lax.fori_loop(0, 2 * RING, step, 0)

    def contract_all(h, buf, take_sems, first_out):
        contract(h, buf, core, True)
        yield
        arrive(buf.at[1 - core, h], take_sems.at[h], place)
        out_hbm = (rows_hbm, errs_hbm)[first_out // 2]
        outs.append(pltpu.make_async_copy(buf.at[:, h], out_hbm.at[:, h], out_sem.at[first_out + h]))
        outs[-1].start()
        contract(h, buf, 1 - core, False)

    def decode(h, mm, x, c):
        cols = pl.ds(pl.multiple_of((x * 2 + c) * BLOCK, BLOCK), BLOCK)
        return nn(act[h], w[mm, :, cols])

    blocked = (2, RING, HALF, BLOCK)

    def half_step(h):
        tokens = pl.ds(h * HALF_TOKENS, HALF_TOKENS)
        yield from gather(place, h, rows, rows_sems, pending)
        yield from contract_all(h, rows, rows_take, 0)
        for i in range(4):
            at = pl.ds(i * 128, 128)
            lat, slope[h, at, :] = gelu_pair(total[h, at, :] + column_of(enc_ref[i : i + 1, :]))
            latsum[h, at, :] = jnp.sum(lat, -1, keepdims=True)
            act_t[at, tokens] = lat.astype(jnp.bfloat16)
            act[h, :, at] = lat.T.astype(jnp.bfloat16)
        yield
        pairs = []
        for k in range(8):
            mm, x = k // 4, k % 4
            give[h, :, mm, :, x] = decode(h, mm, x, 1 - core).astype(jnp.bfloat16).reshape(blocked)
            ref = (h, slice(None), mm, slice(None), x)
            pairs.append(send(give.at[ref], taken.at[ref], pair_send.at[h, k], pair_recv.at[h, k], place.sibling()))
            if k % 4 == 3:
                yield
        for k in range(8):
            mm, x = k // 4, k % 4
            here = decode(h, mm, x, core)
            pairs[k].wait_recv()
            there = taken[h, :, mm, :, x].reshape(HALF_TOKENS, BLOCK).astype(jnp.float32)
            sums[h, :, mm, :, x] = (here + there).astype(jnp.bfloat16).reshape(blocked)
            if k == 3:
                yield
        pending.extend((give.at[h, :, 0, :, 0], pair_send.at[h, k]) for k in range(8))
        yield from scatter_sum(place, h, sums, landing, result, (sum_send, sum_recv), pending)
        bias = dec_ref[pl.ds(m, 1), pl.ds(pl.multiple_of(place.dp * BLOCK, BLOCK), BLOCK)]
        target = own_ref[h * HALF : (h + 1) * HALF, :].astype(jnp.float32)
        errs[(core, h) + own] = (result[h] + bias - target).astype(jnp.bfloat16)
        yield from gather(place, h, errs, errs_sems, pending)
        yield from contract_all(h, errs, errs_take, 2)
        for i in range(4):
            at = pl.ds(i * 128, 128)
            norm_total = norms[0, at, :] + norms[1, at, :]
            pre_grad = (2.0 / TOKENS * total[h, at, :] + sparsity / TOKENS * norm_total) * slope[h, at, :]
            gsum[h, at, :] = jnp.sum(pre_grad, -1, keepdims=True)
            pre_t[at, tokens] = pre_grad.astype(jnp.bfloat16)

    halves = {"a": half_step(0), "b": half_step(1)}
    normed = 0
    for turn in ORDER.split():
        if turn == "n":
            norm_rows(8 * normed, 8)
            normed += 1
        else:
            for _ in range(int(turn[1:])):
                next(halves[turn[0]], None)
    for i in range(4):
        at = pl.ds(i * 128, 128)
        genc_ref[i : i + 1, :] = row_of(gsum[0, at, :] + gsum[1, at, :])
    scale_ref[...] = sparsity / TOKENS * (latsum[0] + latsum[1]) / norms[...]
    for copy in outs:
        copy.wait()
    for ref, sem in pending:
        arrive(ref, sem, place)


def grad_kernel(rows, errs, w, act_t, pre_t, scale, genc, gw, genc_out, gdec):
    ones = jnp.ones((16, TOKENS), jnp.bfloat16)
    for c in (0, 1):
        cols = pl.ds(c * BLOCK, BLOCK)
        for mm in (0, 1):
            err = errs[c, :, :, mm, :, 0].reshape(TOKENS, BLOCK)
            row = rows[c, :, :, mm, :, 0].reshape(TOKENS, BLOCK)
            grad = 2.0 / TOKENS * nn(act_t[...], err) + nn(pre_t[...], row)
            gw[:, mm, cols] = (grad + scale[mm] * w[mm, :, cols].astype(jnp.float32)).astype(jnp.bfloat16)
            gdec[mm : mm + 1, cols] = 2.0 / TOKENS * nn(ones, err)[:1]
    genc_out[...] = genc[...]


def shards(
    residual, norm_gain, w_query, w_key, w_value, w_output, doc_lengths, coder_weight, enc_bias, dec_bias
):
    latents, _, features = coder_weight.shape
    blocks = (2, 2, 2, RING, RING, HALF, BLOCK)
    bf16, f32 = jnp.bfloat16, jnp.float32
    dma, vm = pltpu.SemaphoreType.DMA, pltpu.VMEM
    vmem = pl.BlockSpec(memory_space=pltpu.VMEM)
    hbm = pl.BlockSpec(memory_space=pl.ANY)
    ring = [dma((2, 3)), dma((2, 3, RING)), dma((2,)), dma((2,))]
    half = np.arange(HEAD_DIM // 2)
    freq = np.concatenate([rope_base ** (-half * 2.0 / HEAD_DIM)] * 2)[None].astype(np.float32)
    block = (TOK_DEV, BLOCK)
    rows, errs, w_t, act_t, pre_t, scale, genc = pl.pallas_call(
        step_kernel,
        out_shape=(
            jax.ShapeDtypeStruct((2,) + blocks, bf16),
            jax.ShapeDtypeStruct((2,) + blocks, bf16),
            jax.ShapeDtypeStruct((2, latents, features), bf16),
            jax.ShapeDtypeStruct((latents, TOKENS), bf16),
            jax.ShapeDtypeStruct((latents, TOKENS), bf16),
            jax.ShapeDtypeStruct((2, latents, 1), f32),
            jax.ShapeDtypeStruct((4, 128), f32),
        ),
        in_specs=[vmem] * 6 + [pl.BlockSpec(memory_space=pltpu.SMEM), vmem, hbm, vmem, vmem],
        out_specs=(hbm, hbm, hbm, vmem, vmem, vmem, vmem),
        scratch_shapes=[
            vm((8,) + block, bf16),
            vm((2, RING) + block, bf16),
            vm(block, bf16),
            vm((RING, TOK_DEV, 768), f32),
            vm((RING, TOK_DEV, 768), f32),
            vm((RING, TOK_DEV, 768), f32),
            vm((RING, TOK_DEV, 768), bf16),
            vm((RING, TOK_DEV, 768), bf16),
            vm((8, TOK_DEV, 2 * HEAD_DIM), bf16),
            vm((8,) + block, bf16),
            vm(block, f32),
            vm((8,) + block, bf16),
            vm((8,) + block, bf16),
            vm(block, bf16),
            vm((2,) + blocks, bf16),
            vm((2,) + blocks, bf16),
            vm((2, SPLIT, 2, features), bf16),
            vm((2, latents, features), bf16),
            vm(blocks, bf16),
            vm(blocks, bf16),
            vm(blocks, bf16),
            vm(blocks, bf16),
            vm((2, HALF, BLOCK), f32),
            vm((2, latents, HALF_TOKENS), f32),
            vm((2, HALF_TOKENS, latents), bf16),
            vm((2, latents, HALF_TOKENS), f32),
            vm((2, latents, 1), f32),
            vm((2, latents, 1), f32),
            vm((2, latents, 1), f32),
            *[dma(()), dma(()), dma((8,)), dma(()), dma(()), dma(())],
            *[dma(()), dma(()), dma(()), dma(()), dma(()), dma((8,)), dma(()), dma(())],
            dma((2,)),
            *ring,
            *ring,
            dma((2, 3)),
            dma((2, 3)),
            dma((2, 8)),
            dma((2, 8)),
            dma((5,)),
        ],
        compiler_params=pltpu.CompilerParams(collective_id=0, has_side_effects=True, vmem_limit_bytes=62 * 1024 * 1024),
        cost_estimate=pl.CostEstimate(flops=6 * TOKENS * latents * 2 * features, bytes_accessed=40 << 20, transcendentals=0),
    )(
        residual[0], norm_gain, w_query[0], w_key[0], w_value[0], w_output[0], doc_lengths, jnp.asarray(freq),
        coder_weight, enc_bias.reshape(4, 128), dec_bias,
    )
    set_spec = pl.BlockSpec(
        (2, 2, 2, 2, RING, 1, HALF, BLOCK), lambda k: (0, 0, 0, 0, 0, k, 0, 0)
    )
    whole = lambda *shape: pl.BlockSpec(shape, lambda k: (0,) * len(shape))
    weight_grad, grad_enc, grad_dec = pl.pallas_call(
        grad_kernel,
        grid=(RING,),
        out_shape=(
            jax.ShapeDtypeStruct((latents, 2, features), bf16),
            jax.ShapeDtypeStruct((4, 128), f32),
            jax.ShapeDtypeStruct((2, features), f32),
        ),
        in_specs=[
            set_spec,
            set_spec,
            pl.BlockSpec((2, latents, 2 * BLOCK), lambda k: (0, 0, k)),
            whole(latents, TOKENS),
            whole(latents, TOKENS),
            whole(2, latents, 1),
            whole(4, 128),
        ],
        out_specs=(
            pl.BlockSpec((latents, 2, 2 * BLOCK), lambda k: (0, 0, k)),
            whole(4, 128),
            pl.BlockSpec((2, 2 * BLOCK), lambda k: (0, k)),
        ),
        compiler_params=pltpu.CompilerParams(vmem_limit_bytes=62 * 1024 * 1024),
    )(rows, errs, w_t, act_t, pre_t, scale, genc)
    return (weight_grad, grad_enc.reshape(-1), grad_dec)


def solution(mesh):
    return jax.shard_map(
        shards,
        mesh=mesh,
        in_specs=(
            P("grp", "dp", None),
            P("grp", None),
            P("grp", "dp", "tp"),
            P("grp", "dp", "tp"),
            P("grp", "dp", "tp"),
            P("grp", "tp", "dp"),
            P(),
            P(("grp", "tp", "dp"), None, None),
            P(("grp", "tp", "dp")),
            P(),
        ),
        out_specs=(P(("grp", "tp", "dp"), None, None), P(("grp", "tp", "dp")), P()),
        check_vma=False,
    )
```
